32 devices in a mesh: rows: 8 (over z, y), filt: 4 (over x, core).
Axes of the slice: x: 2, y: 2, z: 4, core: 2. Of those that a mesh axis runs over, the one named last changes fastest.
Arguments:
- features: bfloat16 [512, 8, 512], P('filt', 'rows'), may hold values from -6 to 6
- first_weight: bfloat16 [512, 3, 3, 512], P('filt'), may hold values from -0.09375 to 0.09375
- second_weight: bfloat16 [512, 3, 3, 512], P('filt'), may hold values from -0.09375 to 0.09375
- out_grad: bfloat16 [512, 8, 512], P('filt', 'rows'), may hold values from -0.09375 to 0.09375
Outputs:
- block_out: bfloat16 [512, 8, 512], P('filt', 'rows')
- first_grad: float32 [512, 3, 3, 512], P('filt')
- second_grad: float32 [512, 3, 3, 512], P('filt')
The draws below stay inside these ranges and needn't reach their ends.
All inputs are finite; a program needn't handle non-finite values.
Results may differ from the reference program's by a relative error of at most 0.024.
The reference program's roundings to bfloat16 on the way (of `hidden`, `grad_second` and `grad_first`) count: a program that leaves them out, or rounds other values in their place, can miss the bound.
Values may be sent and summed in bfloat16 or wider, within the bound.
No kernel may reach another device: no remote copies, remote signals or barrier semaphores. Data moves between devices by JAX's collectives and lax.ppermute only.
A program may use at most 64 MiB of HBM per device.

```python
import jax
import jax.numpy as jnp

C = 512
W = 512
ROWS_DEV = 1
H = 8
N_ROWS = 8


def levels(own_key, dims, cuts, smallest, top_value):
    def one(axis_at, parts):
        steps = jax.random.uniform(jax.random.fold_in(jax.random.fold_in(own_key, 6), axis_at), (parts,), jnp.float32, smallest / len(cuts), top_value / len(cuts))
        return jnp.repeat(jnp.exp(steps), dims[axis_at] // parts).reshape((-1,) + (1,) * (len(dims) - axis_at - 1))

    level = one(*cuts[0])
    for cut in cuts[1:]:
        level = level * one(*cut)
    return level


def centred(key, shape, deviation, reach, cuts=(), dtype=jnp.bfloat16):
    entries = deviation * jax.random.normal(key, shape, jnp.float32)
    if cuts:
        entries = entries * levels(key, shape, cuts, -0.22, 0.18)
    return jnp.clip(entries, -reach, reach).astype(dtype)


def setup_inputs(seed: int = 0) -> dict:
    arg_keys = jax.random.split(jax.random.key(seed), 5)
    return {
        "features": centred(arg_keys[0], (C, H, W), 1.0, 6.0, ((0, 4), (1, 8))),
        "first_weight": centred(arg_keys[1], (C, 3, 3, C), (9 * C) ** -0.5, 0.09375, ((0, 4),)),
        "second_weight": centred(arg_keys[2], (C, 3, 3, C), (9 * C) ** -0.5, 0.09375, ((0, 4),)),
        "out_grad": centred(arg_keys[3], (C, H, W), (1.0 / (ROWS_DEV * N_ROWS * W) ** 0.5), 0.09375, ((0, 4), (1, 8))),
    }


def shift_cols(value, offset):
    if offset == 0:
        return value
    if offset > 0:
        return jnp.pad(value[..., offset:], ((0, 0), (0, 0), (0, offset)))
    return jnp.pad(value[..., :offset], ((0, 0), (0, 0), (-offset, 0)))


def conv_forward(weight, padded, count):
    total = jnp.zeros((weight.shape[0], count, padded.shape[2]), jnp.float32)
    for a in range(3):
        for b in range(3):
            part = jnp.einsum("oi,ihw->ohw", weight[:, a, b, :].astype(jnp.float32), padded[:, a:a + count, :].astype(jnp.float32))
            total = total + shift_cols(part, b - 1)
    return total


def conv_backward(weight, padded, count):
    total = jnp.zeros((weight.shape[3], count, padded.shape[2]), jnp.float32)
    for a in range(3):
        for b in range(3):
            part = jnp.einsum("oi,ohw->ihw", weight[:, a, b, :].astype(jnp.float32), padded[:, 2 - a:2 - a + count, :].astype(jnp.float32))
            total = total + shift_cols(part, 1 - b)
    return total


def weight_terms(grad, padded, count):
    rows_out = []
    for a in range(3):
        cols_out = []
        for b in range(3):
            moved = shift_cols(grad, 1 - b)
            cols_out.append(jnp.einsum("ohw,ihw->oi", moved.astype(jnp.float32), padded[:, a:a + count, :].astype(jnp.float32)))
        rows_out.append(jnp.stack(cols_out, axis=1))
    return jnp.stack(rows_out, axis=1)


def pad_rows(value):
    return jnp.pad(value, ((0, 0), (1, 1), (0, 0)))


def reference(features, first_weight, second_weight, out_grad):
    count = features.shape[1]
    padded_in = pad_rows(features)
    pre_first = conv_forward(first_weight, padded_in, count)
    hidden = jnp.maximum(pre_first, 0.0).astype(jnp.bfloat16)
    padded_hidden = pad_rows(hidden)
    pre_second = conv_forward(second_weight, padded_hidden, count) + features.astype(jnp.float32)
    block_out = jnp.maximum(pre_second, 0.0).astype(jnp.bfloat16)
    grad_second = jnp.where(pre_second > 0, out_grad.astype(jnp.float32), 0.0).astype(jnp.bfloat16)
    hidden_grad = conv_backward(second_weight, pad_rows(grad_second), count)
    grad_first = jnp.where(pre_first > 0, hidden_grad, 0.0).astype(jnp.bfloat16)
    second_grad = weight_terms(grad_second, padded_hidden, count)
    first_grad = weight_terms(grad_first, padded_in, count)
    return block_out, first_grad, second_grad
```

```python
import functools

import jax
import jax.numpy as jnp
from jax import lax
from jax.experimental import pallas as pl
from jax.experimental.pallas import tpu as pltpu
from jax.sharding import PartitionSpec as P

BF = jnp.bfloat16
F32 = jnp.float32
VMEM_BYTES = 56 * 1024 * 1024


def extended(cells, sides, width):
    for axis, dim in sides:
        count = lax.axis_size(axis)
        ends = count - 1
        head = lax.slice_in_dim(cells, 0, width, axis=dim)
        tail = lax.slice_in_dim(cells, cells.shape[dim] - width, cells.shape[dim], axis=dim)
        cells = jnp.concatenate(
            [
                lax.ppermute(tail, axis, [(i, (i + 1) % count) for i in range(ends)]),
                cells,
                lax.ppermute(head, axis, [((i + 1) % count, i) for i in range(ends)]),
            ],
            axis=dim,
        )
    return cells


def shift_cols(value, offset):
    if offset == 0:
        return value
    if offset > 0:
        return jnp.pad(value[..., offset:], ((0, 0), (0, 0), (0, offset)))
    return jnp.pad(value[..., :offset], ((0, 0), (0, 0), (-offset, 0)))


def conv_forward(weight, padded, count):
    total = jnp.zeros((weight.shape[0], count, padded.shape[2]), F32)
    for a in range(3):
        for b in range(3):
            part = jnp.einsum(
                "oi,ihw->ohw", weight[:, a, b, :], padded[:, a : a + count, :], preferred_element_type=F32
            )
            total = total + shift_cols(part, b - 1)
    return total


def conv_backward(weight, padded, count):
    total = jnp.zeros((weight.shape[3], count, padded.shape[2]), F32)
    for a in range(3):
        for b in range(3):
            part = jnp.einsum(
                "oi,ohw->ihw", weight[:, a, b, :], padded[:, 2 - a : 2 - a + count, :], preferred_element_type=F32
            )
            total = total + shift_cols(part, 1 - b)
    return total


def weight_terms(grad, padded, count):
    rows_out = []
    for a in range(3):
        cols_out = []
        for b in range(3):
            moved = shift_cols(grad, 1 - b)
            cols_out.append(
                jnp.einsum("ohw,ihw->oi", moved, padded[:, a : a + count, :], preferred_element_type=F32)
            )
        rows_out.append(jnp.stack(cols_out, axis=1))
    return jnp.stack(rows_out, axis=1)


def with_rims(value):
    return extended(value, (("rows", 1),), 1)


def all_channels(value):
    return lax.all_gather(with_rims(value), "filt", axis=0, tiled=True)


def split_rows(features, first_weight, second_weight, out_grad):
    count = features.shape[1]
    padded_in = all_channels(features)
    pre_first = conv_forward(first_weight, padded_in, count)
    hidden = jnp.maximum(pre_first, 0.0).astype(BF)
    padded_hidden = all_channels(hidden)
    pre_second = conv_forward(second_weight, padded_hidden, count) + features.astype(F32)
    block_out = jnp.maximum(pre_second, 0.0).astype(BF)
    grad_second = jnp.where(pre_second > 0, out_grad.astype(F32), 0.0).astype(BF)
    rimmed_grad = with_rims(grad_second)
    terms = conv_backward(second_weight, rimmed_grad, count)
    hidden_grad = lax.psum_scatter(terms, "filt", scatter_dimension=0, tiled=True)
    grad_first = jnp.where(pre_first > 0, hidden_grad, 0.0).astype(BF)
    second_local = weight_terms(grad_second, padded_hidden, count)
    first_local = weight_terms(grad_first, padded_in, count)
    first_grad, second_grad = lax.psum((first_local, second_local), "rows")
    return (block_out, first_grad, second_grad)


def swap(value, axis, bits):
    return lax.ppermute(value, axis, [(i, i ^ bits) for i in range(lax.axis_size(axis))])


def block_at(index, size):
    return pl.ds(pl.multiple_of(index * size, size), size)


def run_copies(copies):
    for c in copies:
        c.start()
    for c in copies:
        c.wait()


def conv_row(weight, x, r):
    acc = jnp.dot(weight[0], x[r], preferred_element_type=F32)
    acc += jnp.dot(weight[1], x[r + 1], preferred_element_type=F32)
    acc += jnp.dot(weight[2], x[r + 2], preferred_element_type=F32)
    return acc


def join_cols(left, mid, right):
    w = mid.shape[1]
    col = lax.broadcasted_iota(jnp.int32, mid.shape, 1)
    out = mid + jnp.where(col == 0, 0.0, pltpu.roll(left, 1, 1))
    return out + jnp.where(col == w - 1, 0.0, pltpu.roll(right, w - 1, 1))


def clear_rims(x):
    x[0] = jnp.zeros(x.shape[1:], x.dtype)
    x[x.shape[0] - 1] = jnp.zeros(x.shape[1:], x.dtype)


def first_kernel(places, n_pieces, *refs):
    pieces, weight = refs[:n_pieces], refs[n_pieces]
    full, hidden, mask, x, sems, out_sem = refs[n_pieces + 1 :]
    rows, own = hidden.shape[0], hidden.shape[1]
    r0, f0 = lax.axis_index("rows"), lax.axis_index("filt")
    copies = []
    for (piece, k, d, e, lo), ref in zip(places, [pieces[p[0]] for p in places]):
        size = ref.shape[1]
        at = pl.multiple_of((f0 ^ e) * own + lo, 16)
        copies.append(
            pltpu.make_async_copy(ref.at[k], x.at[1 + (r0 ^ d), pl.ds(at, size)], sems.at[len(copies)])
        )
    for c in copies:
        c.start()
    clear_rims(x)
    for c in copies:
        c.wait()
    out = pltpu.make_async_copy(x.at[pl.ds(1, rows)], full, out_sem)
    out.start()

    def step(r, carry):
        acc = conv_row(weight, x, r)
        pre = join_cols(acc[:own], acc[own : 2 * own], acc[2 * own :])
        hidden[r] = jnp.maximum(pre, 0.0).astype(BF)
        mask[r] = jnp.where(pre > 0, 1.0, 0.0).astype(BF)
        return carry

    lax.fori_loop(0, rows, step, 0)
    out.wait()


def load_filt(pieces, x, sems, own):
    f0 = lax.axis_index("filt")
    rows = pieces[0].shape[0]
    return [
        pltpu.make_async_copy(ref, x.at[pl.ds(1, rows), block_at(f0 ^ e, own)], sems.at[e])
        for e, ref in enumerate(pieces)
    ]


def second_kernel(places, n_grad, *refs):
    pieces, full, grads, weight = refs[:4], refs[4], refs[5 : 5 + n_grad], refs[5 + n_grad]
    block_out, grad_second, x, feat, grad, sems, sems_g = refs[6 + n_grad :]
    rows, own = grad_second.shape[0], grad_second.shape[1]
    r0, f0 = lax.axis_index("rows"), lax.axis_index("filt")
    copies = load_filt(pieces, x, sems, own)
    copies.append(pltpu.make_async_copy(full.at[:, block_at(f0, own)], feat, sems.at[4]))
    for n, (piece, k, d) in enumerate(places):
        copies.append(pltpu.make_async_copy(grads[piece].at[k], grad.at[r0 ^ d], sems_g.at[n]))
    for c in copies:
        c.start()
    clear_rims(x)
    for c in copies:
        c.wait()

    def step(r, carry):
        acc = conv_row(weight, x, r)
        pre = join_cols(acc[:own], acc[own : 2 * own], acc[2 * own :]) + feat[r].astype(F32)
        grad_second[r] = jnp.where(pre > 0, grad[r].astype(F32), 0.0).astype(BF)

        @pl.when(r == r0)
        def _():
            block_out[0] = jnp.maximum(pre, 0.0).astype(BF)

        return carry

    lax.fori_loop(0, rows, step, 0)


def turn_kernel(weight, *outs):
    own = weight.shape[1]
    f0 = lax.axis_index("filt")
    for e, out in enumerate(outs):
        for t in range(weight.shape[0]):
            out[t] = weight[t, :, block_at(f0 ^ e, own)].T


def back_kernel(*refs):
    pieces, turned, mask, grad_first, x, weight, sems, sems_w = refs[:4], refs[4:8], *refs[8:]
    rows, own = grad_first.shape[0], grad_first.shape[1]
    f0 = lax.axis_index("filt")
    copies = load_filt(pieces, x, sems, own)
    for e, ref in enumerate(turned):
        copies.append(pltpu.make_async_copy(ref, weight.at[:, :, block_at(f0 ^ e, own)], sems_w.at[e]))
    for c in copies:
        c.start()
    clear_rims(x)
    for c in copies:
        c.wait()
    c = weight.shape[2]

    def step(r, carry):
        acc = None
        for a in range(3):
            lhs = weight[3 * a : 3 * a + 3].reshape(3 * own, c)
            part = jnp.dot(lhs, x[r + 2 - a], preferred_element_type=F32)
            acc = part if acc is None else acc + part
        total = join_cols(acc[2 * own :], acc[own : 2 * own], acc[:own])
        grad_first[r] = jnp.where(mask[r] > 0, total, 0.0).astype(BF)
        return carry

    lax.fori_loop(0, rows, step, 0)


def fill_moved(grad, moved):
    rows, own, w = grad.shape
    clear_rims(moved)
    col = lax.broadcasted_iota(jnp.int32, (own, w), 1)

    def step(r, carry):
        g = grad[r].astype(F32)
        moved[r + 1, 0:own] = jnp.where(col == w - 1, 0.0, pltpu.roll(g, w - 1, 1)).astype(BF)
        moved[r + 1, own : 2 * own] = grad[r]
        moved[r + 1, 2 * own :] = jnp.where(col == 0, 0.0, pltpu.roll(g, 1, 1)).astype(BF)
        return carry

    lax.fori_loop(0, rows, step, 0)


def sum_terms(moved, x, first, out):
    rows, taps = moved.shape[0] - 2, moved.shape[1]
    for a in range(3):

        def step(h, acc, a=a):
            return acc + lax.dot_general(
                moved[h - a + 2], x[first + h], (((1,), (1,)), ((), ())), preferred_element_type=F32
            )

        out[a] = lax.fori_loop(0, rows, step, jnp.zeros((taps, x.shape[1]), F32))


def second_terms_kernel(*refs):
    pieces, grad, out, x, moved, sems = refs[:4], *refs[4:]
    copies = load_filt(pieces, x, sems, grad.shape[1])
    for c in copies:
        c.start()
    fill_moved(grad, moved)
    for c in copies:
        c.wait()
    sum_terms(moved, x, 1, out)


def first_terms_kernel(full, grad, out, x, moved, sem):
    copy = pltpu.make_async_copy(full, x, sem)
    copy.start()
    fill_moved(grad, moved)
    copy.wait()
    sum_terms(moved, x, 0, out)


ANY = pl.BlockSpec(memory_space=pl.ANY)
VM = pl.BlockSpec(memory_space=pltpu.VMEM)


def call(kernel, ins, outs, scratch, flops, name):
    nbytes = sum(v.size * v.dtype.itemsize for v, _ in ins)
    return pl.pallas_call(
        kernel,
        out_shape=[jax.ShapeDtypeStruct(s, d) for s, d, _ in outs],
        in_specs=[s for _, s in ins],
        out_specs=[s for _, _, s in outs],
        scratch_shapes=scratch,
        compiler_params=pltpu.CompilerParams(vmem_limit_bytes=VMEM_BYTES),
        cost_estimate=pl.CostEstimate(flops=flops, bytes_accessed=nbytes, transcendentals=0),
        name=name,
    )(*[v for v, _ in ins])


def all_rows(features, first_weight, second_weight, out_grad):
    c = first_weight.shape[3]
    own, _, w = features.shape
    rows = lax.axis_size("rows")
    flops = 2 * 9 * own * c * w * rows
    dma = pltpu.SemaphoreType.DMA
    feat = jnp.transpose(features, (1, 0, 2))
    ograd = jnp.transpose(out_grad, (1, 0, 2))
    w1 = jnp.transpose(first_weight, (1, 2, 0, 3)).reshape(3, 3 * own, c)
    w2 = jnp.transpose(second_weight, (1, 2, 0, 3))

    zs = tuple(range(0, rows, 2))
    own_z = jnp.concatenate([feat] + [swap(feat, "rows", d) for d in zs[1:]], axis=0)
    half = own // 2
    over_x = swap(own_z, "filt", 2)
    over_y = swap(own_z, "rows", 1)
    diag_lo = swap(over_x[:, :half], "rows", 1)
    diag_hi = swap(over_y[:, half:], "filt", 2)
    mine = [own_z, over_x, over_y, diag_lo, diag_hi]
    moves = [(0, 0, 0), (0, 2, 0), (1, 0, 0), (1, 2, 0), (1, 2, half)]
    pieces, places = [], []
    for core in (0, 1):
        for value, (d, e, lo) in zip(mine, moves):
            for k, z in enumerate(zs):
                places.append((len(pieces), k, z ^ d, e ^ core, lo))
            pieces.append(swap(value, "filt", 1) if core else value)
    full, hidden, mask = call(
        functools.partial(first_kernel, places, len(pieces)),
        [(v, ANY) for v in pieces] + [(w1, VM)],
        [((rows, c, w), BF, ANY), ((rows, own, w), BF, VM), ((rows, own, w), BF, VM)],
        [pltpu.VMEM((rows + 2, c, w), BF), dma((len(places),)), dma],
        flops,
        "first_conv",
    )

    grad_z = jnp.concatenate([ograd] + [swap(ograd, "rows", d) for d in zs[1:]], axis=0)
    grads = [grad_z, swap(grad_z, "rows", 1)]
    grad_places = [(p, k, z ^ p) for p in (0, 1) for k, z in enumerate(zs)]

    w2_blocks = w2.reshape(9, own, c)
    turned = call(
        turn_kernel, [(w2_blocks, VM)], [((9, own, own), BF, VM)] * 4, [], 0, "turn_weight"
    )
    turned = [turned[0]] + [swap(turned[e], "filt", e) for e in (1, 2, 3)]

    def over_filt(value):
        far = swap(value, "filt", 2)
        return [value, swap(value, "filt", 1), far, swap(far, "filt", 1)]

    hiddens = over_filt(hidden)
    block_out, grad_second = call(
        functools.partial(second_kernel, grad_places, len(grads)),
        [(v, ANY) for v in hiddens + [full] + grads] + [(w2.reshape(3, 3 * own, c), VM)],
        [((1, own, w), BF, VM), ((rows, own, w), BF, VM)],
        [
            pltpu.VMEM((rows + 2, c, w), BF),
            pltpu.VMEM((rows, own, w), BF),
            pltpu.VMEM((rows, own, w), BF),
            dma((5,)),
            dma((len(grad_places),)),
        ],
        flops,
        "second_conv",
    )
    seconds = over_filt(grad_second)
    (second_grad,) = call(
        second_terms_kernel,
        [(v, ANY) for v in hiddens] + [(grad_second, VM)],
        [((3, 3 * own, c), F32, VM)],
        [pltpu.VMEM((rows + 2, c, w), BF), pltpu.VMEM((rows + 2, 3 * own, w), BF), dma((4,))],
        flops,
        "second_terms",
    )
    (grad_first,) = call(
        back_kernel,
        [(v, ANY) for v in seconds + turned] + [(mask, VM)],
        [((rows, own, w), BF, VM)],
        [pltpu.VMEM((rows + 2, c, w), BF), pltpu.VMEM((9, own, c), BF), dma((4,)), dma((4,))],
        flops,
        "hidden_grad",
    )
    (first_grad,) = call(
        first_terms_kernel,
        [(full, ANY), (grad_first, VM)],
        [((3, 3 * own, c), F32, VM)],
        [pltpu.VMEM((rows, c, w), BF), pltpu.VMEM((rows + 2, 3 * own, w), BF), dma],
        flops,
        "first_terms",
    )

    def as_weight(value):
        return jnp.transpose(value.reshape(3, 3, own, c), (2, 0, 1, 3))

    return jnp.transpose(block_out, (1, 0, 2)), as_weight(first_grad), as_weight(second_grad)


def solution(mesh):
    in_specs = (
        P("filt", "rows", None),
        P("filt", None, None, None),
        P("filt", None, None, None),
        P("filt", "rows", None),
    )
    out_specs = (P("filt", "rows", None), P("filt", None, None, None), P("filt", None, None, None))

    def per_device(features, first_weight, second_weight, out_grad):
        rows, filt = mesh.shape["rows"], mesh.shape["filt"]
        small = rows == 8 and filt == 4 and features.shape[1] == 1 and features.shape[0] % 32 == 0
        plan = all_rows if small else split_rows
        return plan(features, first_weight, second_weight, out_grad)

    return jax.shard_map(per_device, mesh=mesh, in_specs=in_specs, out_specs=out_specs, check_vma=False)
```

```python
import functools

import jax
import jax.numpy as jnp
from jax import lax
from jax.experimental import pallas as pl
from jax.experimental.pallas import tpu as pltpu
from jax.sharding import PartitionSpec as P

BF = jnp.bfloat16
F32 = jnp.float32
VMEM_BYTES = 24 * 1024 * 1024


def extended(cells, sides, width):
    for axis, dim in sides:
        count = lax.axis_size(axis)
        ends = count - 1
        head = lax.slice_in_dim(cells, 0, width, axis=dim)
        tail = lax.slice_in_dim(cells, cells.shape[dim] - width, cells.shape[dim], axis=dim)
        cells = jnp.concatenate(
            [
                lax.ppermute(tail, axis, [(i, (i + 1) % count) for i in range(ends)]),
                cells,
                lax.ppermute(head, axis, [((i + 1) % count, i) for i in range(ends)]),
            ],
            axis=dim,
        )
    return cells


def shift_cols(value, offset):
    if offset == 0:
        return value
    if offset > 0:
        return jnp.pad(value[..., offset:], ((0, 0), (0, 0), (0, offset)))
    return jnp.pad(value[..., :offset], ((0, 0), (0, 0), (-offset, 0)))


def conv_forward(weight, padded, count):
    total = jnp.zeros((weight.shape[0], count, padded.shape[2]), F32)
    for a in range(3):
        for b in range(3):
            part = jnp.einsum(
                "oi,ihw->ohw", weight[:, a, b, :], padded[:, a : a + count, :], preferred_element_type=F32
            )
            total = total + shift_cols(part, b - 1)
    return total


def conv_backward(weight, padded, count):
    total = jnp.zeros((weight.shape[3], count, padded.shape[2]), F32)
    for a in range(3):
        for b in range(3):
            part = jnp.einsum(
                "oi,ohw->ihw", weight[:, a, b, :], padded[:, 2 - a : 2 - a + count, :], preferred_element_type=F32
            )
            total = total + shift_cols(part, 1 - b)
    return total


def weight_terms(grad, padded, count):
    rows_out = []
    for a in range(3):
        cols_out = []
        for b in range(3):
            moved = shift_cols(grad, 1 - b)
            cols_out.append(
                jnp.einsum("ohw,ihw->oi", moved, padded[:, a : a + count, :], preferred_element_type=F32)
            )
        rows_out.append(jnp.stack(cols_out, axis=1))
    return jnp.stack(rows_out, axis=1)


def with_rims(value):
    return extended(value, (("rows", 1),), 1)


def all_channels(value):
    return lax.all_gather(with_rims(value), "filt", axis=0, tiled=True)


def split_rows(features, first_weight, second_weight, out_grad):
    count = features.shape[1]
    padded_in = all_channels(features)
    pre_first = conv_forward(first_weight, padded_in, count)
    hidden = jnp.maximum(pre_first, 0.0).astype(BF)
    padded_hidden = all_channels(hidden)
    pre_second = conv_forward(second_weight, padded_hidden, count) + features.astype(F32)
    block_out = jnp.maximum(pre_second, 0.0).astype(BF)
    grad_second = jnp.where(pre_second > 0, out_grad.astype(F32), 0.0).astype(BF)
    rimmed_grad = with_rims(grad_second)
    terms = conv_backward(second_weight, rimmed_grad, count)
    hidden_grad = lax.psum_scatter(terms, "filt", scatter_dimension=0, tiled=True)
    grad_first = jnp.where(pre_first > 0, hidden_grad, 0.0).astype(BF)
    second_local = weight_terms(grad_second, padded_hidden, count)
    first_local = weight_terms(grad_first, padded_in, count)
    first_grad, second_grad = lax.psum((first_local, second_local), "rows")
    return (block_out, first_grad, second_grad)


def swap(value, axis, bits):
    return lax.ppermute(value, axis, [(i, i ^ bits) for i in range(lax.axis_size(axis))])


def block_at(index, size):
    return pl.ds(pl.multiple_of(index * size, size), size)


def join_cols(left, mid, right):
    w = mid.shape[1]
    col = lax.broadcasted_iota(jnp.int32, mid.shape, 1)
    out = mid + jnp.where(col == 0, 0.0, pltpu.roll(left, 1, 1))
    return out + jnp.where(col == w - 1, 0.0, pltpu.roll(right, w - 1, 1))


def window(weight, x, r, rows, lo):
    c, w = x.shape[1], x.shape[2]
    first, last = max(r - 1, 0), min(r + 1, rows - 1)
    lhs = weight[:, (first - r + 1) * c : (last - r + 2) * c]
    rhs = x[first - lo : last - lo + 1].reshape((last - first + 1) * c, w)
    return jnp.dot(lhs, rhs, preferred_element_type=F32)


def thirds(acc):
    own = acc.shape[0] // 3
    return acc[:own], acc[own : 2 * own], acc[2 * own :]


def widen(weight, wide):
    c = weight.shape[2]
    for a in range(3):
        wide[:, a * c : (a + 1) * c] = weight[a]


def gather_rows(full, places, pieces):
    own = pieces[0].shape[1]
    r0, f0 = lax.axis_index("rows"), lax.axis_index("filt")
    for piece, k, d, e, lo in places:
        size = pieces[piece].shape[1]
        at = pl.ds(pl.multiple_of((f0 ^ e) * own + lo, size), size)
        full[r0 ^ d, at] = pieces[piece][k]


def first_rows(part, full, wide, hidden, mask):
    for r in range(*part):
        pre = join_cols(*thirds(window(wide, full, r, full.shape[0], 0)))
        hidden[r - part[0]] = jnp.maximum(pre, 0.0).astype(BF)
        mask[r - part[0]] = jnp.where(pre > 0, 1.0, 0.0).astype(BF)


def store_early(early, value, n, y0):
    count = early.shape[0]

    @pl.when(y0 == n // count)
    def _():
        early[n % count] = value


def first_kernel(places, n_pieces, part, *refs):
    pieces, weight = refs[:n_pieces], refs[n_pieces]
    full, hidden, mask, wide = refs[n_pieces + 1 :]
    gather_rows(full, places, pieces)
    widen(weight, wide)
    first_rows(part, full, wide, hidden, mask)


def first_rest_kernel(part, full, weight, hidden, mask, wide):
    widen(weight, wide)
    first_rows(part, full, wide, hidden, mask)


def copy_pieces(layout, refs, put, lo, hi):
    y0, f0 = lax.axis_index("rows") & 1, lax.axis_index("filt")
    for (e, base, kind), ref in zip(layout, refs):
        count, own = ref.shape[:2]
        at = block_at(f0 ^ e, own)
        for n in range(count):
            if kind == "whole":
                if lo <= base + n < hi:
                    put(base + n, at, ref[n])
                continue
            half = y0 if kind == "own" else 1 - y0
            for y in (0, 1):
                if lo <= base + y * count + n < hi:

                    @pl.when(half == y)
                    def _(ref=ref, n=n, y=y, at=at):
                        put(base + y * count + n, at, ref[n])


def fill_rows(x, layout, refs, lo, hi):
    def put(r, at, value):
        x[r - lo, at] = value

    copy_pieces(layout, refs, put, lo, hi)


def second_kernel(grad_places, layout, n_grad, part, rows, *refs):
    pieces, refs = refs[: len(layout)], refs[len(layout) :]
    full, grads, weight, before = refs[0], refs[1 : 1 + n_grad], refs[1 + n_grad], refs[2 + n_grad]
    block_out, grad_second, *early, wide, x, grad = refs[3 + n_grad :]
    own = grad_second.shape[1]
    r0, f0 = lax.axis_index("rows"), lax.axis_index("filt")
    y0 = r0 & 1
    lo, hi = max(part[0] - 1, 0), min(part[1] + 1, rows)
    fill_rows(x, layout, pieces, lo, hi)
    for piece, k, d in grad_places:
        grad[r0 ^ d] = grads[piece][k]
    widen(weight, wide)
    block_out[...] = before[...]
    for r in range(*part):
        feat = full[r, block_at(f0, own)].astype(F32)
        pre = join_cols(*thirds(window(wide, x, r, rows, lo))) + feat
        value = jnp.where(pre > 0, grad[r].astype(F32), 0.0).astype(BF)
        grad_second[r - part[0]] = value
        if early:
            store_early(early[0], value, r - part[0], y0)

        @pl.when(r0 == r)
        def _(pre=pre):
            block_out[0] = jnp.maximum(pre, 0.0).astype(BF)


def turn_kernel(weight, mine, mate, over):
    taps, own = weight.shape[:2]
    f0, y0 = lax.axis_index("filt"), lax.axis_index("rows") & 1
    for t in range(taps):
        mine[t] = weight[t, :, block_at(f0, own)].T
        mate[t] = weight[t, :, block_at(f0 ^ 1, own)].T
        for e in (2, 3):
            block = weight[t, :, block_at(f0 ^ e, own)].T

            @pl.when(y0 == 0)
            def _(block=block, e=e, t=t):
                over[e - 2, t] = block[: own // 2]

            @pl.when(y0 == 1)
            def _(block=block, e=e, t=t):
                over[e - 2, t] = block[own // 2 :]


def back_kernel(layout, *refs):
    pieces = refs[: len(layout)]
    mine, mate, near2, far2, near3, far3, mask_a, mask_b, grad_first, wide, x = refs[len(layout) :]
    rows, own = grad_first.shape[:2]
    c = x.shape[1]
    f0, y0 = lax.axis_index("filt"), lax.axis_index("rows") & 1
    fill_rows(x, layout, pieces, 0, rows)
    for t in range(9):
        a, b = t // 3, t % 3

        def at(e, a=a):
            return pl.ds(pl.multiple_of((2 - a) * c + (f0 ^ e) * own, own), own)

        wide[b * own : (b + 1) * own, at(0)] = mine[t]
        wide[b * own : (b + 1) * own, at(1)] = mate[t]
        for e, near, far in ((2, near2, far2), (3, near3, far3)):
            for y, ref in ((y0, near), (1 - y0, far)):
                rows_at = pl.ds(pl.multiple_of(b * own + y * (own // 2), own // 2), own // 2)
                wide[rows_at, at(e)] = ref[0, t]
    cut = mask_a.shape[0]
    for r in range(rows):
        left, mid, right = thirds(window(wide, x, r, rows, 0))
        total = join_cols(right, mid, left)
        mask = mask_a[r] if r < cut else mask_b[r - cut]
        grad_first[r] = jnp.where(mask > 0, total, 0.0).astype(BF)


def fill_moved(grads, moved):
    own, w = grads[0].shape[1:]
    col = lax.broadcasted_iota(jnp.int32, (own, w), 1)
    for r, (grad, n) in enumerate((grad, n) for grad in grads for n in range(grad.shape[0])):
        g = grad[n].astype(F32)
        at = slice(r * w, (r + 1) * w)
        moved[0:own, at] = jnp.where(col == w - 1, 0.0, pltpu.roll(g, w - 1, 1)).astype(BF)
        moved[own : 2 * own, at] = grad[n]
        moved[2 * own :, at] = jnp.where(col == 0, 0.0, pltpu.roll(g, 1, 1)).astype(BF)


def sum_terms(moved, x, w, out):
    n = moved.shape[1]
    for a, (m, h) in enumerate([(slice(w, n), slice(0, n - w)), (slice(0, n),) * 2, (slice(0, n - w), slice(w, n))]):
        out[a] = lax.dot_general(moved[:, m], x[:, h], (((1,), (1,)), ((), ())), preferred_element_type=F32)


def second_terms_kernel(layout, *refs):
    pieces, (grad_a, grad_b, out, x, moved) = refs[: len(layout)], refs[len(layout) :]
    w = grad_a.shape[2]

    def put(r, at, value):
        x[at, r * w : (r + 1) * w] = value

    copy_pieces(layout, pieces, put, 0, moved.shape[1] // w)
    fill_moved([grad_a, grad_b], moved)
    sum_terms(moved, x, w, out)


def first_terms_kernel(n_grads, full, *refs):
    grads, (out, x, moved) = refs[:n_grads], refs[n_grads:]
    rows, _, w = full.shape
    for r in range(rows):
        x[:, r * w : (r + 1) * w] = full[r]
    fill_moved(grads, moved)
    sum_terms(moved, x, w, out)


VM = pl.BlockSpec(memory_space=pltpu.VMEM)


def call(kernel, ins, outs, scratch, flops, name):
    nbytes = sum(v.size * v.dtype.itemsize for v in ins) if flops else 0
    return pl.pallas_call(
        kernel,
        out_shape=[jax.ShapeDtypeStruct(s, d) for s, d in outs],
        in_specs=[VM] * len(ins),
        out_specs=[VM] * len(outs),
        scratch_shapes=scratch,
        compiler_params=pltpu.CompilerParams(vmem_limit_bytes=VMEM_BYTES),
        cost_estimate=pl.CostEstimate(flops=flops, bytes_accessed=nbytes, transcendentals=0),
        name=name,
    )(*ins)


def wave(values):
    return dict(zip(values, lax.optimization_barrier(tuple(values.values()))))


def over_x(value):
    return swap(value, "filt", 2)


def over_y(value):
    return swap(value, "rows", 1)


def to_mate(value):
    return swap(value, "filt", 1)


def all_rows(features, first_weight, second_weight, out_grad):
    c = first_weight.shape[3]
    own, _, w = features.shape
    rows = lax.axis_size("rows")
    half, cut = own // 2, rows // 2
    row_flops = 2 * 9 * own * c * w
    vm = pltpu.VMEM
    zs = tuple(range(2, rows, 2))
    wide = vm((3 * own, 3 * c), BF)
    w1 = jnp.transpose(first_weight, (1, 2, 0, 3)).reshape(3, 3 * own, c)
    w2 = jnp.transpose(second_weight, (1, 2, 0, 3))
    w2_wide = w2.reshape(3, 3 * own, c)
    feat = jnp.transpose(features, (1, 0, 2))
    ograd = jnp.transpose(out_grad, (1, 0, 2))

    def act(n):
        return ((n, own, w), BF)

    v = {f"z{d}": swap(feat, "rows", d) for d in zs}
    mine, mate, over = call(
        turn_kernel,
        [w2.reshape(9, own, c)],
        [((9, own, own), BF), ((9, own, own), BF), ((2, 9, half, own), BF)],
        [],
        row_flops * 2,
        "turn_weight",
    )
    v |= {"mine": mine, "mate": mate, "near": over_x(over)}
    v = wave(v)

    zs = (0, *zs)
    z4 = jnp.concatenate([feat] + [v[f"z{d}"] for d in zs[1:]], axis=0)
    v |= {f"g{d}": swap(ograd, "rows", d) for d in zs[1:]}
    v |= {"z4": z4, "x4": over_x(z4), "y4": over_y(z4)}
    v = wave(v)

    v |= {"lo": over_y(v["x4"][:, :half]), "hi": over_x(v["y4"][:, half:])}
    v |= {"m" + k: to_mate(v[k]) for k in ("z4", "x4", "y4")}
    v |= {"g4": jnp.concatenate([ograd] + [v[f"g{d}"] for d in zs[1:]], axis=0)}
    v = wave(v)
    v |= {"mlo": to_mate(v["lo"]), "mhi": to_mate(v["hi"])}
    v = wave(v)

    pieces, places = [], []
    for name, d, e, lo in (("z4", 0, 0, 0), ("x4", 0, 2, 0), ("y4", 1, 0, 0), ("lo", 1, 2, 0), ("hi", 1, 2, half)):
        for core in (0, 1):
            places += [(len(pieces), k, z ^ d, e ^ core, lo) for k, z in enumerate(zs)]
            pieces.append(v["m" * core + name])
    cut_a, cut = rows // 2 + 1, rows // 2
    full, h_a, mask_a = call(
        functools.partial(first_kernel, places, len(pieces), (0, cut_a)),
        pieces + [w1],
        [((rows, c, w), BF), act(cut_a), act(cut_a)],
        [wide],
        0,
        "first_conv_a",
    )
    h = {"a0": h_a, "a1": to_mate(h_a), "a2": over_x(h_a)}
    gy = over_y(v["g4"])
    h |= {"m1": to_mate(v["mate"]), "near3": to_mate(v["near"][1:])}
    h["b0"], mask_b = call(
        functools.partial(first_rest_kernel, (cut_a, rows)),
        [full, w1],
        [act(rows - cut_a)] * 2,
        [wide],
        0,
        "first_conv_b",
    )
    h = wave(h)
    h |= {"b2": over_x(h["b0"]), "b1": to_mate(h["b0"])}
    a3 = to_mate(h["a2"])
    layout_a = [(e, 0, "whole") for e in range(4)]
    spread_a = [h["a0"], h["a1"], h["a2"], a3]
    grads = [v["g4"], gy]
    grad_places = [(p, k, z ^ p) for p in (0, 1) for k, z in enumerate(zs)]

    def second(layout, spread, part, before, early, name):
        n = part[1] - part[0]
        return call(
            functools.partial(second_kernel, grad_places, layout, len(grads), part, rows),
            [*spread, full, *grads, w2_wide, before],
            [act(1), act(n)] + [act(n // 2)] * early,
            [wide, vm((min(part[1] + 1, rows) - max(part[0] - 1, 0), c, w), BF), vm((rows, own, w), BF)],
            0,
            name,
        )

    s = {"b0": h["b0"], "b1": h["b1"], "b2": h["b2"], "far": over_y(lax.optimization_barrier((v["near"], gy))[0])}
    s["out"], s["a0"], s["early"] = second(layout_a, spread_a, (0, cut), feat, 1, "second_conv_a")
    s = wave(s)
    layout_b = layout_a + [(e, cut_a, "whole") for e in range(4)]
    spread_b = spread_a + [s["b0"], s["b1"], s["b2"], to_mate(s["b2"])]
    t = {"a0": s["a0"], "s2": over_x(s["early"]), "a1": to_mate(s["a0"])}
    t["out"], t["b0"] = second(layout_b, spread_b, (cut, rows), s["out"], 0, "second_conv_b")
    t = wave(t)
    t |= {"b2": over_x(t["b0"]), "t2": over_y(t["s2"]), "b1": to_mate(t["b0"]), "s3": to_mate(t["s2"])}
    t |= {"far3": to_mate(s["far"][1:])}
    (t["grad"],) = call(
        functools.partial(second_terms_kernel, layout_b),
        [*spread_b, t["a0"], t["b0"]],
        [((3, 3 * own, c), F32)],
        [vm((c, rows * w), BF), vm((3 * own, rows * w), BF)],
        row_flops * rows,
        "second_terms",
    )
    t = wave(t)
    t |= {"b3": to_mate(t["b2"]), "t3": to_mate(t["t2"])}
    t = wave(t)
    layout = [(e, 0, "whole") for e in (0, 1)] + [(e, cut, "whole") for e in range(4)]
    layout += [(e, 0, kind) for kind in ("own", "other") for e in (2, 3)]
    turned = [v["mine"], h["m1"], v["near"][:1], s["far"][:1], h["near3"], t["far3"]]
    (grad_first,) = call(
        functools.partial(back_kernel, layout),
        [*(t[k] for k in ("a0", "a1", "b0", "b1", "b2", "b3", "s2", "s3", "t2", "t3")), *turned, mask_a, mask_b],
        [act(rows)],
        [wide, vm((rows, c, w), BF)],
        row_flops * rows,
        "hidden_grad",
    )
    (first_grad,) = call(
        functools.partial(first_terms_kernel, 1),
        [full, grad_first],
        [((3, 3 * own, c), F32)],
        [vm((c, rows * w), BF), vm((3 * own, rows * w), BF)],
        row_flops * rows,
        "first_terms",
    )

    def as_weight(value):
        return jnp.transpose(value.reshape(3, 3, own, c), (2, 0, 1, 3))

    return jnp.transpose(t["out"], (1, 0, 2)), as_weight(first_grad), as_weight(t["grad"])


def solution(mesh):
    in_specs = (
        P("filt", "rows", None),
        P("filt", None, None, None),
        P("filt", None, None, None),
        P("filt", "rows", None),
    )
    out_specs = (P("filt", "rows", None), P("filt", None, None, None), P("filt", None, None, None))

    def per_device(features, first_weight, second_weight, out_grad):
        rows, filt = mesh.shape["rows"], mesh.shape["filt"]
        small = rows == 8 and filt == 4 and features.shape[1] == 1 and features.shape[0] % 32 == 0
        plan = all_rows if small else split_rows
        return plan(features, first_weight, second_weight, out_grad)

    return jax.shard_map(per_device, mesh=mesh, in_specs=in_specs, out_specs=out_specs, check_vma=False)
```

```python
import functools

import jax
import jax.numpy as jnp
from jax import lax
from jax.experimental import pallas as pl
from jax.experimental.pallas import tpu as pltpu
from jax.sharding import PartitionSpec as P

BF = jnp.bfloat16
F32 = jnp.float32
VMEM_BYTES = 24 * 1024 * 1024


def extended(cells, sides, width):
    for axis, dim in sides:
        count = lax.axis_size(axis)
        ends = count - 1
        head = lax.slice_in_dim(cells, 0, width, axis=dim)
        tail = lax.slice_in_dim(cells, cells.shape[dim] - width, cells.shape[dim], axis=dim)
        cells = jnp.concatenate(
            [
                lax.ppermute(tail, axis, [(i, (i + 1) % count) for i in range(ends)]),
                cells,
                lax.ppermute(head, axis, [((i + 1) % count, i) for i in range(ends)]),
            ],
            axis=dim,
        )
    return cells


def shift_cols(value, offset):
    if offset == 0:
        return value
    if offset > 0:
        return jnp.pad(value[..., offset:], ((0, 0), (0, 0), (0, offset)))
    return jnp.pad(value[..., :offset], ((0, 0), (0, 0), (-offset, 0)))


def conv_forward(weight, padded, count):
    total = jnp.zeros((weight.shape[0], count, padded.shape[2]), F32)
    for a in range(3):
        for b in range(3):
            part = jnp.einsum(
                "oi,ihw->ohw", weight[:, a, b, :], padded[:, a : a + count, :], preferred_element_type=F32
            )
            total = total + shift_cols(part, b - 1)
    return total


def conv_backward(weight, padded, count):
    total = jnp.zeros((weight.shape[3], count, padded.shape[2]), F32)
    for a in range(3):
        for b in range(3):
            part = jnp.einsum(
                "oi,ohw->ihw", weight[:, a, b, :], padded[:, 2 - a : 2 - a + count, :], preferred_element_type=F32
            )
            total = total + shift_cols(part, 1 - b)
    return total


def weight_terms(grad, padded, count):
    rows_out = []
    for a in range(3):
        cols_out = []
        for b in range(3):
            moved = shift_cols(grad, 1 - b)
            cols_out.append(
                jnp.einsum("ohw,ihw->oi", moved, padded[:, a : a + count, :], preferred_element_type=F32)
            )
        rows_out.append(jnp.stack(cols_out, axis=1))
    return jnp.stack(rows_out, axis=1)


def with_rims(value):
    return extended(value, (("rows", 1),), 1)


def all_channels(value):
    return lax.all_gather(with_rims(value), "filt", axis=0, tiled=True)


def split_rows(features, first_weight, second_weight, out_grad):
    count = features.shape[1]
    padded_in = all_channels(features)
    pre_first = conv_forward(first_weight, padded_in, count)
    hidden = jnp.maximum(pre_first, 0.0).astype(BF)
    padded_hidden = all_channels(hidden)
    pre_second = conv_forward(second_weight, padded_hidden, count) + features.astype(F32)
    block_out = jnp.maximum(pre_second, 0.0).astype(BF)
    grad_second = jnp.where(pre_second > 0, out_grad.astype(F32), 0.0).astype(BF)
    rimmed_grad = with_rims(grad_second)
    terms = conv_backward(second_weight, rimmed_grad, count)
    hidden_grad = lax.psum_scatter(terms, "filt", scatter_dimension=0, tiled=True)
    grad_first = jnp.where(pre_first > 0, hidden_grad, 0.0).astype(BF)
    second_local = weight_terms(grad_second, padded_hidden, count)
    first_local = weight_terms(grad_first, padded_in, count)
    first_grad, second_grad = lax.psum((first_local, second_local), "rows")
    return (block_out, first_grad, second_grad)


def swap(value, axis, bits):
    return lax.ppermute(value, axis, [(i, i ^ bits) for i in range(lax.axis_size(axis))])


def block_at(index, size):
    return pl.ds(pl.multiple_of(index * size, size), size)


def join_cols(left, mid, right):
    w = mid.shape[1]
    col = lax.broadcasted_iota(jnp.int32, mid.shape, 1)
    out = mid + jnp.where(col == 0, 0.0, pltpu.roll(left, 1, 1))
    return out + jnp.where(col == w - 1, 0.0, pltpu.roll(right, w - 1, 1))


def window(weight, x, r, rows, lo):
    c, w = x.shape[1], x.shape[2]
    first, last = max(r - 1, 0), min(r + 1, rows - 1)
    lhs = weight[:, (first - r + 1) * c : (last - r + 2) * c]
    rhs = x[first - lo : last - lo + 1].reshape((last - first + 1) * c, w)
    return jnp.dot(lhs, rhs, preferred_element_type=F32)


def thirds(acc):
    own = acc.shape[0] // 3
    return acc[:own], acc[own : 2 * own], acc[2 * own :]


def widen(weight, wide):
    c = weight.shape[2]
    for a in range(3):
        wide[:, a * c : (a + 1) * c] = weight[a]


def gather_rows(full, places, pieces):
    own = pieces[0].shape[1]
    r0, f0 = lax.axis_index("rows"), lax.axis_index("filt")
    for piece, k, d, e, lo in places:
        size = pieces[piece].shape[1]
        at = pl.ds(pl.multiple_of((f0 ^ e) * own + lo, size), size)
        full[r0 ^ d, at] = pieces[piece][k]


def first_rows(part, full, wide, hidden, mask):
    for r in range(*part):
        pre = join_cols(*thirds(window(wide, full, r, full.shape[0], 0)))
        hidden[r - part[0]] = jnp.maximum(pre, 0.0).astype(BF)
        mask[r - part[0]] = jnp.where(pre > 0, 1.0, 0.0).astype(BF)


def store_early(early, value, n, y0):
    count = early.shape[0]

    @pl.when(y0 == n // count)
    def _():
        early[n % count] = value


def first_kernel(places, n_pieces, part, *refs):
    pieces, weight = refs[:n_pieces], refs[n_pieces]
    full, hidden, mask, wide = refs[n_pieces + 1 :]
    gather_rows(full, places, pieces)
    widen(weight, wide)
    first_rows(part, full, wide, hidden, mask)


def first_rest_kernel(part, full, weight, hidden, mask, flat, wide):
    widen(weight, wide)
    first_rows(part, full, wide, hidden, mask)
    rows, _, w = full.shape
    for r in range(rows):
        flat[:, r * w : (r + 1) * w] = full[r]


def copy_pieces(layout, refs, put, lo, hi):
    y0, f0 = lax.axis_index("rows") & 1, lax.axis_index("filt")
    for (e, base, kind), ref in zip(layout, refs):
        count, own = ref.shape[:2]
        at = block_at(f0 ^ e, own)
        for n in range(count):
            if kind == "whole":
                if lo <= base + n < hi:
                    put(base + n, at, ref[n])
                continue
            half = y0 if kind == "own" else 1 - y0
            for y in (0, 1):
                if lo <= base + y * count + n < hi:

                    @pl.when(half == y)
                    def _(ref=ref, n=n, y=y, at=at):
                        put(base + y * count + n, at, ref[n])


def fill_rows(x, layout, refs, lo, hi):
    def put(r, at, value):
        x[r - lo, at] = value

    copy_pieces(layout, refs, put, lo, hi)


def second_kernel(grad_places, layout, n_grad, part, rows, *refs):
    pieces, refs = refs[: len(layout)], refs[len(layout) :]
    full, grads, weight, before = refs[0], refs[1 : 1 + n_grad], refs[1 + n_grad], refs[2 + n_grad]
    block_out, grad_second, *early, wide, x, grad = refs[3 + n_grad :]
    own = grad_second.shape[1]
    r0, f0 = lax.axis_index("rows"), lax.axis_index("filt")
    y0 = r0 & 1
    lo, hi = max(part[0] - 1, 0), min(part[1] + 1, rows)
    fill_rows(x, layout, pieces, lo, hi)
    for piece, k, d in grad_places:
        grad[r0 ^ d] = grads[piece][k]
    widen(weight, wide)
    block_out[...] = before[...]
    for r in range(*part):
        feat = full[r, block_at(f0, own)].astype(F32)
        pre = join_cols(*thirds(window(wide, x, r, rows, lo))) + feat
        value = jnp.where(pre > 0, grad[r].astype(F32), 0.0).astype(BF)
        grad_second[r - part[0]] = value
        if early:
            store_early(early[0], value, r - part[0], y0)

        @pl.when(r0 == r)
        def _(pre=pre):
            block_out[0] = jnp.maximum(pre, 0.0).astype(BF)


def turn_kernel(weight, mine, mate, over):
    taps, own = weight.shape[:2]
    f0, y0 = lax.axis_index("filt"), lax.axis_index("rows") & 1
    for t in range(taps):
        mine[t] = weight[t, :, block_at(f0, own)].T
        mate[t] = weight[t, :, block_at(f0 ^ 1, own)].T
        for e in (2, 3):
            block = weight[t, :, block_at(f0 ^ e, own)].T

            @pl.when(y0 == 0)
            def _(block=block, e=e, t=t):
                over[e - 2, t] = block[: own // 2]

            @pl.when(y0 == 1)
            def _(block=block, e=e, t=t):
                over[e - 2, t] = block[own // 2 :]


def back_rows(part, rows, lo, x, wide, masks, grad_first):
    for r in range(*part):
        left, mid, right = thirds(window(wide, x, r, rows, lo))
        total = join_cols(right, mid, left)
        (mask,) = [ref[r - base] for base, ref in masks if 0 <= r - base < ref.shape[0]]
        grad_first[r - part[0]] = jnp.where(mask > 0, total, 0.0).astype(BF)


def back_kernel(layout, part, rows, *refs):
    pieces = refs[: len(layout)]
    mine, mate, near2, far2, near3, far3, mask, grad_first, wide, x = refs[len(layout) :]
    own, c = grad_first.shape[1], x.shape[1]
    f0, y0 = lax.axis_index("filt"), lax.axis_index("rows") & 1
    lo, hi = max(part[0] - 1, 0), min(part[1] + 1, rows)
    fill_rows(x, layout, pieces, lo, hi)
    for t in range(9):
        a, b = t // 3, t % 3

        def at(e, a=a):
            return pl.ds(pl.multiple_of((2 - a) * c + (f0 ^ e) * own, own), own)

        wide[b * own : (b + 1) * own, at(0)] = mine[t]
        wide[b * own : (b + 1) * own, at(1)] = mate[t]
        for e, near, far in ((2, near2, far2), (3, near3, far3)):
            for y, ref in ((y0, near), (1 - y0, far)):
                rows_at = pl.ds(pl.multiple_of(b * own + y * (own // 2), own // 2), own // 2)
                wide[rows_at, at(e)] = ref[0, t]
    back_rows(part, rows, lo, x, wide, [(0, mask)], grad_first)


def back_rest_kernel(layout, part, rows, cut, *refs):
    pieces, (wide, mask_a, mask_b, grad_first, x) = refs[: len(layout)], refs[len(layout) :]
    lo, hi = max(part[0] - 1, 0), min(part[1] + 1, rows)
    fill_rows(x, layout, pieces, lo, hi)
    back_rows(part, rows, lo, x, wide, [(0, mask_a), (cut, mask_b)], grad_first)


def fill_moved(grads, moved):
    own, w = grads[0].shape[1:]
    col = lax.broadcasted_iota(jnp.int32, (own, w), 1)
    for r, (grad, n) in enumerate((grad, n) for grad in grads for n in range(grad.shape[0])):
        g = grad[n].astype(F32)
        at = slice(r * w, (r + 1) * w)
        moved[0:own, at] = jnp.where(col == w - 1, 0.0, pltpu.roll(g, w - 1, 1)).astype(BF)
        moved[own : 2 * own, at] = grad[n]
        moved[2 * own :, at] = jnp.where(col == 0, 0.0, pltpu.roll(g, 1, 1)).astype(BF)


def sum_terms(moved, x, w, a, part):
    rows = x.shape[1] // w
    lo, hi = max(part[0], 1 - a), min(part[1], rows + 1 - a)
    left, right = moved[:, (lo - part[0]) * w : (hi - part[0]) * w], x[:, (lo + a - 1) * w : (hi + a - 1) * w]
    return lax.dot_general(left, right, (((1,), (1,)), ((), ())), preferred_element_type=F32)


def second_terms_kernel(layout, *refs):
    pieces, (grad_a, grad_b, out, x, moved) = refs[: len(layout)], refs[len(layout) :]
    w = grad_a.shape[2]
    rows = moved.shape[1] // w

    def put(r, at, value):
        x[at, r * w : (r + 1) * w] = value

    copy_pieces(layout, pieces, put, 0, rows)
    fill_moved([grad_a, grad_b], moved)
    for a in range(3):
        out[a] = sum_terms(moved, x, w, a, (0, rows))


def first_terms_kernel(part, flat, grad, out, moved):
    fill_moved([grad], moved)
    for a in range(3):
        out[a] = sum_terms(moved, flat, grad.shape[2], a, part)


def first_terms_rest_kernel(part, flat, grad, before, out, moved, total, sems):
    fill_moved([grad], moved)
    copies = []
    for a in range(3):
        total[a] = before[a] + sum_terms(moved, flat, grad.shape[2], a, part)
        copies.append(pltpu.make_async_copy(total.at[a], out.at[a], sems.at[a]))
        copies[-1].start()
    for copy in copies:
        copy.wait()


VM = pl.BlockSpec(memory_space=pltpu.VMEM)


def call(kernel, ins, outs, scratch, flops, name, out_spec=VM):
    nbytes = sum(v.size * v.dtype.itemsize for v in ins) if flops else 0
    return pl.pallas_call(
        kernel,
        out_shape=[jax.ShapeDtypeStruct(s, d) for s, d in outs],
        in_specs=[VM] * len(ins),
        out_specs=[out_spec] * len(outs),
        scratch_shapes=scratch,
        compiler_params=pltpu.CompilerParams(vmem_limit_bytes=VMEM_BYTES),
        cost_estimate=pl.CostEstimate(flops=flops, bytes_accessed=nbytes, transcendentals=0),
        name=name,
    )(*ins)


def wave(values):
    return dict(zip(values, lax.optimization_barrier(tuple(values.values()))))


def over_x(value):
    return swap(value, "filt", 2)


def over_y(value):
    return swap(value, "rows", 1)


def to_mate(value):
    return swap(value, "filt", 1)


def all_rows(features, first_weight, second_weight, out_grad):
    c = first_weight.shape[3]
    own, _, w = features.shape
    rows = lax.axis_size("rows")
    half, cut = own // 2, rows // 2
    row_flops = 2 * 9 * own * c * w
    vm = pltpu.VMEM
    zs = tuple(range(2, rows, 2))
    wide = vm((3 * own, 3 * c), BF)
    w1 = jnp.transpose(first_weight, (1, 2, 0, 3)).reshape(3, 3 * own, c)
    w2 = jnp.transpose(second_weight, (1, 2, 0, 3))
    w2_wide = w2.reshape(3, 3 * own, c)
    feat = jnp.transpose(features, (1, 0, 2))
    ograd = jnp.transpose(out_grad, (1, 0, 2))

    def act(n):
        return ((n, own, w), BF)

    v = {f"z{d}": swap(feat, "rows", d) for d in zs}
    mine, mate, over = call(
        turn_kernel,
        [w2.reshape(9, own, c)],
        [((9, own, own), BF), ((9, own, own), BF), ((2, 9, half, own), BF)],
        [],
        row_flops * 2,
        "turn_weight",
    )
    v |= {"mine": mine, "mate": mate, "near": over_x(over)}
    v = wave(v)

    zs = (0, *zs)
    z4 = jnp.concatenate([feat] + [v[f"z{d}"] for d in zs[1:]], axis=0)
    v |= {f"g{d}": swap(ograd, "rows", d) for d in zs[1:]}
    v |= {"z4": z4, "x4": over_x(z4), "y4": over_y(z4)}
    v = wave(v)

    v |= {"lo": over_y(v["x4"][:, :half]), "hi": over_x(v["y4"][:, half:])}
    v |= {"m" + k: to_mate(v[k]) for k in ("z4", "x4", "y4")}
    v |= {"g4": jnp.concatenate([ograd] + [v[f"g{d}"] for d in zs[1:]], axis=0)}
    v = wave(v)
    v |= {"mlo": to_mate(v["lo"]), "mhi": to_mate(v["hi"])}
    v = wave(v)

    pieces, places = [], []
    for name, d, e, lo in (("z4", 0, 0, 0), ("x4", 0, 2, 0), ("y4", 1, 0, 0), ("lo", 1, 2, 0), ("hi", 1, 2, half)):
        for core in (0, 1):
            places += [(len(pieces), k, z ^ d, e ^ core, lo) for k, z in enumerate(zs)]
            pieces.append(v["m" * core + name])
    cut_a, cut = rows // 2 + 1, rows // 2
    full, h_a, mask_a = call(
        functools.partial(first_kernel, places, len(pieces), (0, cut_a)),
        pieces + [w1],
        [((rows, c, w), BF), act(cut_a), act(cut_a)],
        [wide],
        0,
        "first_conv_a",
    )
    h = {"a0": h_a, "a1": to_mate(h_a), "a2": over_x(h_a)}
    gy = over_y(v["g4"])
    h |= {"m1": to_mate(v["mate"]), "near3": to_mate(v["near"][1:])}
    h["b0"], mask_b, flat = call(
        functools.partial(first_rest_kernel, (cut_a, rows)),
        [full, w1],
        [act(rows - cut_a)] * 2 + [((c, rows * w), BF)],
        [wide],
        0,
        "first_conv_b",
    )
    h = wave(h)
    h |= {"b2": over_x(h["b0"]), "b1": to_mate(h["b0"])}
    a3 = to_mate(h["a2"])
    layout_a = [(e, 0, "whole") for e in range(4)]
    spread_a = [h["a0"], h["a1"], h["a2"], a3]
    grads = [v["g4"], gy]
    grad_places = [(p, k, z ^ p) for p in (0, 1) for k, z in enumerate(zs)]

    def second(layout, spread, part, before, early, name):
        n = part[1] - part[0]
        return call(
            functools.partial(second_kernel, grad_places, layout, len(grads), part, rows),
            [*spread, full, *grads, w2_wide, before],
            [act(1), act(n)] + [act(n // 2)] * early,
            [wide, vm((min(part[1] + 1, rows) - max(part[0] - 1, 0), c, w), BF), vm((rows, own, w), BF)],
            0,
            name,
        )

    s = {"b0": h["b0"], "b1": h["b1"], "b2": h["b2"], "far": over_y(lax.optimization_barrier((v["near"], gy))[0])}
    s["out"], s["a0"], s["early"] = second(layout_a, spread_a, (0, cut), feat, 1, "second_conv_a")
    s = wave(s)
    layout_b = layout_a + [(e, cut_a, "whole") for e in range(4)]
    spread_b = spread_a + [s["b0"], s["b1"], s["b2"], to_mate(s["b2"])]
    t = {"a0": s["a0"], "s2": over_x(s["early"]), "a1": to_mate(s["a0"]), "far3": to_mate(s["far"][1:])}
    t["out"], t["b0"] = second(layout_b, spread_b, (cut, rows), s["out"], 0, "second_conv_b")
    t = wave(t)
    b2 = over_x(t["b0"])
    t |= {"b1": to_mate(t["b0"]), "t2": over_y(t["s2"]), "s3": to_mate(t["s2"])}

    (second_grad,) = call(
        functools.partial(second_terms_kernel, layout_b),
        [*spread_b, t["a0"], t["b0"]],
        [((3, 3 * own, c), F32)],
        [vm((c, rows * w), BF), vm((3 * own, rows * w), BF)],
        0,
        "second_terms",
    )
    t["t2"], second_grad = lax.optimization_barrier((t["t2"], second_grad))
    t["t3"] = to_mate(t["t2"])
    last = cut - 1
    layout = [(e, 0, "whole") for e in (0, 1)] + [(e, 0, kind) for kind in ("own", "other") for e in (2, 3)]
    names = ["a0", "a1", "s2", "s3", "t2", "t3"]
    turned = [v["mine"], h["m1"], v["near"][:1], s["far"][:1], h["near3"], t["far3"]]
    grad_first, wide_back = call(
        functools.partial(back_kernel, layout, (0, last), rows),
        [*(t[k] for k in names), *turned, mask_a],
        [act(last), ((3 * own, 3 * c), BF)],
        [vm((cut, c, w), BF)],
        0,
        "hidden_grad_a",
    )
    (terms,) = call(
        functools.partial(first_terms_kernel, (0, last)),
        [flat, grad_first],
        [((3, 3 * own, c), F32)],
        [vm((3 * own, last * w), BF)],
        0,
        "first_terms_a",
    )
    t |= {"b2": b2, "terms": terms, "wide": wide_back, "grad": second_grad}
    t = wave(t)
    layout += [(e, cut, "whole") for e in range(4)]
    (grad_first,) = call(
        functools.partial(back_rest_kernel, layout, (last, rows), rows, cut_a),
        [*(t[k] for k in names), t["b0"], t["b1"], t["b2"], to_mate(t["b2"]), t["wide"], mask_a, mask_b],
        [act(rows - last)],
        [vm((rows - last + 1, c, w), BF)],
        row_flops * (rows - last),
        "hidden_grad_b",
    )
    (first_grad,) = call(
        functools.partial(first_terms_rest_kernel, (last, rows)),
        [flat, grad_first, t["terms"]],
        [((3, 3 * own, c), F32)],
        [vm((3 * own, (rows - last) * w), BF), vm((3, 3 * own, c), F32), pltpu.SemaphoreType.DMA((3,))],
        row_flops * (rows - last),
        "first_terms_b",
        pl.BlockSpec(memory_space=pl.ANY),
    )

    def as_weight(value):
        return jnp.transpose(value.reshape(3, 3, own, c), (2, 0, 1, 3))

    return jnp.transpose(t["out"], (1, 0, 2)), as_weight(first_grad), as_weight(t["grad"])


def solution(mesh):
    in_specs = (
        P("filt", "rows", None),
        P("filt", None, None, None),
        P("filt", None, None, None),
        P("filt", "rows", None),
    )
    out_specs = (P("filt", "rows", None), P("filt", None, None, None), P("filt", None, None, None))

    def per_device(features, first_weight, second_weight, out_grad):
        rows, filt = mesh.shape["rows"], mesh.shape["filt"]
        small = rows == 8 and filt == 4 and features.shape[1] == 1 and features.shape[0] % 32 == 0
        plan = all_rows if small else split_rows
        return plan(features, first_weight, second_weight, out_grad)

    return jax.shard_map(per_device, mesh=mesh, in_specs=in_specs, out_specs=out_specs, check_vma=False)
```

```python
import functools

import jax
import jax.numpy as jnp
from jax import lax
from jax.experimental import pallas as pl
from jax.experimental.pallas import tpu as pltpu
from jax.sharding import PartitionSpec as P

BF = jnp.bfloat16
F32 = jnp.float32
VMEM_BYTES = 24 * 1024 * 1024


def extended(cells, sides, width):
    for axis, dim in sides:
        count = lax.axis_size(axis)
        ends = count - 1
        head = lax.slice_in_dim(cells, 0, width, axis=dim)
        tail = lax.slice_in_dim(cells, cells.shape[dim] - width, cells.shape[dim], axis=dim)
        cells = jnp.concatenate(
            [
                lax.ppermute(tail, axis, [(i, (i + 1) % count) for i in range(ends)]),
                cells,
                lax.ppermute(head, axis, [((i + 1) % count, i) for i in range(ends)]),
            ],
            axis=dim,
        )
    return cells


def shift_cols(value, offset):
    if offset == 0:
        return value
    if offset > 0:
        return jnp.pad(value[..., offset:], ((0, 0), (0, 0), (0, offset)))
    return jnp.pad(value[..., :offset], ((0, 0), (0, 0), (-offset, 0)))


def conv_forward(weight, padded, count):
    total = jnp.zeros((weight.shape[0], count, padded.shape[2]), F32)
    for a in range(3):
        for b in range(3):
            part = jnp.einsum(
                "oi,ihw->ohw", weight[:, a, b, :], padded[:, a : a + count, :], preferred_element_type=F32
            )
            total = total + shift_cols(part, b - 1)
    return total


def conv_backward(weight, padded, count):
    total = jnp.zeros((weight.shape[3], count, padded.shape[2]), F32)
    for a in range(3):
        for b in range(3):
            part = jnp.einsum(
                "oi,ohw->ihw", weight[:, a, b, :], padded[:, 2 - a : 2 - a + count, :], preferred_element_type=F32
            )
            total = total + shift_cols(part, 1 - b)
    return total


def weight_terms(grad, padded, count):
    rows_out = []
    for a in range(3):
        cols_out = []
        for b in range(3):
            moved = shift_cols(grad, 1 - b)
            cols_out.append(
                jnp.einsum("ohw,ihw->oi", moved, padded[:, a : a + count, :], preferred_element_type=F32)
            )
        rows_out.append(jnp.stack(cols_out, axis=1))
    return jnp.stack(rows_out, axis=1)


def with_rims(value):
    return extended(value, (("rows", 1),), 1)


def all_channels(value):
    return lax.all_gather(with_rims(value), "filt", axis=0, tiled=True)


def split_rows(features, first_weight, second_weight, out_grad):
    count = features.shape[1]
    padded_in = all_channels(features)
    pre_first = conv_forward(first_weight, padded_in, count)
    hidden = jnp.maximum(pre_first, 0.0).astype(BF)
    padded_hidden = all_channels(hidden)
    pre_second = conv_forward(second_weight, padded_hidden, count) + features.astype(F32)
    block_out = jnp.maximum(pre_second, 0.0).astype(BF)
    grad_second = jnp.where(pre_second > 0, out_grad.astype(F32), 0.0).astype(BF)
    rimmed_grad = with_rims(grad_second)
    terms = conv_backward(second_weight, rimmed_grad, count)
    hidden_grad = lax.psum_scatter(terms, "filt", scatter_dimension=0, tiled=True)
    grad_first = jnp.where(pre_first > 0, hidden_grad, 0.0).astype(BF)
    second_local = weight_terms(grad_second, padded_hidden, count)
    first_local = weight_terms(grad_first, padded_in, count)
    first_grad, second_grad = lax.psum((first_local, second_local), "rows")
    return (block_out, first_grad, second_grad)


def swap(value, axis, bits):
    if axis == "filt":
        way = "mate" if bits == 1 else "over_x"
    else:
        way = "over_y" if bits == 1 else "along_z"
    with jax.named_scope(way):
        return lax.ppermute(value, axis, [(i, i ^ bits) for i in range(lax.axis_size(axis))])


def block_at(index, size):
    return pl.ds(pl.multiple_of(index * size, size), size)


def join_cols(left, mid, right):
    w = mid.shape[1]
    col = lax.broadcasted_iota(jnp.int32, mid.shape, 1)
    out = mid + jnp.where(col == 0, 0.0, pltpu.roll(left, 1, 1))
    return out + jnp.where(col == w - 1, 0.0, pltpu.roll(right, w - 1, 1))


def window(weight, x, r, rows, lo):
    c, w = x.shape[1], x.shape[2]
    first, last = max(r - 1, 0), min(r + 1, rows - 1)
    lhs = weight[:, (first - r + 1) * c : (last - r + 2) * c]
    rhs = x[first - lo : last - lo + 1].reshape((last - first + 1) * c, w)
    return jnp.dot(lhs, rhs, preferred_element_type=F32)


def thirds(acc):
    own = acc.shape[0] // 3
    return acc[:own], acc[own : 2 * own], acc[2 * own :]


def widen(weight, wide):
    c = weight.shape[2]
    for a in range(3):
        wide[:, a * c : (a + 1) * c] = weight[a]


def gather_rows(full, places, pieces):
    own = pieces[0].shape[1]
    r0, f0 = lax.axis_index("rows"), lax.axis_index("filt")
    for piece, k, d, e, lo in places:
        size = pieces[piece].shape[1]
        at = pl.ds(pl.multiple_of((f0 ^ e) * own + lo, size), size)
        full[r0 ^ d, at] = pieces[piece][k]


def first_rows(part, full, wide, hidden, mask):
    for r in range(*part):
        pre = join_cols(*thirds(window(wide, full, r, full.shape[0], 0)))
        hidden[r - part[0]] = jnp.maximum(pre, 0.0).astype(BF)
        mask[r - part[0]] = jnp.where(pre > 0, 1.0, 0.0).astype(BF)


def store_early(early, value, n, y0):
    count = early.shape[0]

    @pl.when(y0 == n // count)
    def _():
        early[n % count] = value


def first_kernel(places, n_pieces, part, *refs):
    pieces, weight = refs[:n_pieces], refs[n_pieces]
    full, hidden, mask, wide = refs[n_pieces + 1 :]
    gather_rows(full, places, pieces)
    widen(weight, wide)
    first_rows(part, full, wide, hidden, mask)


def first_rest_kernel(part, full, weight, hidden, mask, flat, wide):
    widen(weight, wide)
    first_rows(part, full, wide, hidden, mask)
    rows, _, w = full.shape
    for r in range(rows):
        flat[:, r * w : (r + 1) * w] = full[r]


def copy_pieces(layout, refs, put, lo, hi):
    y0, f0 = lax.axis_index("rows") & 1, lax.axis_index("filt")
    for (e, base, kind), ref in zip(layout, refs):
        count, own = ref.shape[:2]
        at = block_at(f0 ^ e, own)
        for n in range(count):
            if kind == "whole":
                if lo <= base + n < hi:
                    put(base + n, at, ref[n])
                continue
            half = y0 if kind == "own" else 1 - y0
            for y in (0, 1):
                if lo <= base + y * count + n < hi:

                    @pl.when(half == y)
                    def _(ref=ref, n=n, y=y, at=at):
                        put(base + y * count + n, at, ref[n])


def fill_rows(x, layout, refs, lo, hi):
    def put(r, at, value):
        x[r - lo, at] = value

    copy_pieces(layout, refs, put, lo, hi)


def second_kernel(grad_places, layout, n_grad, part, rows, *refs):
    pieces, refs = refs[: len(layout)], refs[len(layout) :]
    full, grads, weight, before = refs[0], refs[1 : 1 + n_grad], refs[1 + n_grad], refs[2 + n_grad]
    block_out, grad_second, *early, wide, x, grad = refs[3 + n_grad :]
    own = grad_second.shape[1]
    r0, f0 = lax.axis_index("rows"), lax.axis_index("filt")
    y0 = r0 & 1
    lo, hi = max(part[0] - 1, 0), min(part[1] + 1, rows)
    fill_rows(x, layout, pieces, lo, hi)
    for piece, k, d in grad_places:
        grad[r0 ^ d] = grads[piece][k]
    widen(weight, wide)
    block_out[...] = before[...]
    for r in range(*part):
        feat = full[r, block_at(f0, own)].astype(F32)
        pre = join_cols(*thirds(window(wide, x, r, rows, lo))) + feat
        value = jnp.where(pre > 0, grad[r].astype(F32), 0.0).astype(BF)
        grad_second[r - part[0]] = value
        if early:
            store_early(early[0], value, r - part[0], y0)

        @pl.when(r0 == r)
        def _(pre=pre):
            block_out[0] = jnp.maximum(pre, 0.0).astype(BF)


def pick_kernel(weight, mate, over, sems):
    own, half = mate.shape[1], over.shape[2]
    f0, y0 = lax.axis_index("filt"), lax.axis_index("rows") & 1
    copies = [pltpu.make_async_copy(weight.at[:, :, block_at(f0 ^ 1, own)], mate, sems.at[0])]
    for e in (2, 3):
        part = weight.at[:, block_at(y0, half), block_at(f0 ^ e, own)]
        copies.append(pltpu.make_async_copy(part, over.at[e - 2], sems.at[e - 1]))
    for copy in copies:
        copy.start()
    for copy in copies:
        copy.wait()


def turn_kernel(weight, mate, near2, near3, far2, far3, wide):
    own, half = mate.shape[1], near2.shape[2]
    c = wide.shape[1] // 3
    f0, y0 = lax.axis_index("filt"), lax.axis_index("rows") & 1
    for t in range(weight.shape[0]):
        a, b = t // 3, t % 3
        left = jnp.concatenate([near2[0, t], far2[0, t]], axis=0), jnp.concatenate([near3[0, t], far3[0, t]], axis=0)
        right = jnp.concatenate([far2[0, t], near2[0, t]], axis=0), jnp.concatenate([far3[0, t], near3[0, t]], axis=0)
        blocks = [weight[t, :, block_at(f0, own)], mate[t]]
        blocks += [jnp.where(y0 == 0, x, y) for x, y in zip(left, right)]
        for e, block in enumerate(blocks):
            at = pl.ds(pl.multiple_of((2 - a) * c + (f0 ^ e) * own, own), own)
            wide[b * own : (b + 1) * own, at] = block.T


def back_rows(part, rows, lo, x, wide, masks, grad_first):
    for r in range(*part):
        left, mid, right = thirds(window(wide, x, r, rows, lo))
        total = join_cols(right, mid, left)
        (mask,) = [ref[r - base] for base, ref in masks if 0 <= r - base < ref.shape[0]]
        grad_first[r - part[0]] = jnp.where(mask > 0, total, 0.0).astype(BF)


def back_kernel(layout, part, rows, bases, *refs):
    pieces, (wide, *masks, grad_first, x) = refs[: len(layout)], refs[len(layout) :]
    lo, hi = max(part[0] - 1, 0), min(part[1] + 1, rows)
    fill_rows(x, layout, pieces, lo, hi)
    back_rows(part, rows, lo, x, wide, list(zip(bases, masks)), grad_first)


def fill_moved(grads, moved):
    own, w = grads[0].shape[1:]
    col = lax.broadcasted_iota(jnp.int32, (own, w), 1)
    for r, (grad, n) in enumerate((grad, n) for grad in grads for n in range(grad.shape[0])):
        g = grad[n].astype(F32)
        at = slice(r * w, (r + 1) * w)
        moved[0:own, at] = jnp.where(col == w - 1, 0.0, pltpu.roll(g, w - 1, 1)).astype(BF)
        moved[own : 2 * own, at] = grad[n]
        moved[2 * own :, at] = jnp.where(col == 0, 0.0, pltpu.roll(g, 1, 1)).astype(BF)


def sum_terms(moved, x, w, a, part):
    rows = x.shape[1] // w
    lo, hi = max(part[0], 1 - a), min(part[1], rows + 1 - a)
    left, right = moved[:, (lo - part[0]) * w : (hi - part[0]) * w], x[:, (lo + a - 1) * w : (hi + a - 1) * w]
    return lax.dot_general(left, right, (((1,), (1,)), ((), ())), preferred_element_type=F32)


def second_terms_kernel(layout, part, with_before, *refs):
    pieces, (grad, *refs) = refs[: len(layout)], refs[len(layout) :]
    out, x, moved = refs[with_before:]
    w = grad.shape[2]

    def put(r, at, value):
        x[at, r * w : (r + 1) * w] = value

    copy_pieces(layout, pieces, put, max(part[0] - 1, 0), min(part[1] + 1, x.shape[1] // w))
    fill_moved([grad], moved)
    for a in range(3):
        terms = sum_terms(moved, x, w, a, part)
        out[a] = refs[0][a] + terms if with_before else terms


def first_terms_kernel(part, flat, grad, out, moved):
    fill_moved([grad], moved)
    for a in range(3):
        out[a] = sum_terms(moved, flat, grad.shape[2], a, part)


def first_terms_rest_kernel(part, flat, grad, before, out, moved, total, sems):
    fill_moved([grad], moved)
    copies = []
    for a in range(3):
        total[a] = before[a] + sum_terms(moved, flat, grad.shape[2], a, part)
        copies.append(pltpu.make_async_copy(total.at[a], out.at[a], sems.at[a]))
        copies[-1].start()
    for copy in copies:
        copy.wait()


VM = pl.BlockSpec(memory_space=pltpu.VMEM)
ANY = pl.BlockSpec(memory_space=pl.ANY)
DMA = pltpu.SemaphoreType.DMA


def call(kernel, ins, outs, scratch, flops, name, in_spec=VM, out_spec=VM):
    nbytes = sum(v.size * v.dtype.itemsize for v in ins) if flops else 0
    return pl.pallas_call(
        kernel,
        out_shape=[jax.ShapeDtypeStruct(s, d) for s, d in outs],
        in_specs=[in_spec] * len(ins),
        out_specs=[out_spec] * len(outs),
        scratch_shapes=scratch,
        compiler_params=pltpu.CompilerParams(vmem_limit_bytes=VMEM_BYTES),
        cost_estimate=pl.CostEstimate(flops=flops, bytes_accessed=nbytes, transcendentals=0),
        name=name,
    )(*ins)


def wave(values):
    return dict(zip(values, lax.optimization_barrier(tuple(values.values()))))


def over_x(value):
    return swap(value, "filt", 2)


def over_y(value):
    return swap(value, "rows", 1)


def to_mate(value):
    return swap(value, "filt", 1)


def all_rows(features, first_weight, second_weight, out_grad):
    c = first_weight.shape[3]
    own, _, w = features.shape
    rows = lax.axis_size("rows")
    half, cut = own // 2, rows // 2
    row_flops = 2 * 9 * own * c * w
    vm = pltpu.VMEM
    zs = tuple(range(2, rows, 2))
    wide = vm((3 * own, 3 * c), BF)
    w1 = jnp.transpose(first_weight, (1, 2, 0, 3)).reshape(3, 3 * own, c)
    w2 = jnp.transpose(second_weight, (1, 2, 0, 3))
    w2_wide = w2.reshape(3, 3 * own, c)
    feat = jnp.transpose(features, (1, 0, 2))
    ograd = jnp.transpose(out_grad, (1, 0, 2))

    def act(n):
        return ((n, own, w), BF)

    v = {f"z{d}": swap(feat, "rows", d) for d in zs[::-1]}
    w2_taps = w2.reshape(9, own, c)
    mate, over = call(
        pick_kernel,
        [w2_taps],
        [((9, own, own), BF), ((2, 9, half, own), BF)],
        [DMA((3,))],
        0,
        "pick_weight",
        in_spec=ANY,
    )
    v |= {"mate": mate, "near": over_x(over)}
    v = wave(v)

    zs = (0, *zs)
    z4 = jnp.concatenate([feat] + [v[f"z{d}"] for d in zs[1:]], axis=0)
    v |= {f"g{d}": swap(ograd, "rows", d) for d in zs[:0:-1]}
    v |= {"z4": z4, "x4": over_x(z4), "y4": over_y(z4)}
    v = wave(v)

    v |= {"lo": over_y(v["x4"][:, :half]), "hi": over_x(v["y4"][:, half:])}
    v |= {"m" + k: to_mate(v[k]) for k in ("z4", "x4", "y4")}
    v |= {"g4": jnp.concatenate([ograd] + [v[f"g{d}"] for d in zs[1:]], axis=0)}
    v = wave(v)
    v |= {"mlo": to_mate(v["lo"]), "mhi": to_mate(v["hi"])}
    v = wave(v)

    pieces, places = [], []
    for name, d, e, lo in (("z4", 0, 0, 0), ("x4", 0, 2, 0), ("y4", 1, 0, 0), ("lo", 1, 2, 0), ("hi", 1, 2, half)):
        for core in (0, 1):
            places += [(len(pieces), k, z ^ d, e ^ core, lo) for k, z in enumerate(zs)]
            pieces.append(v["m" * core + name])
    cut_a, cut = rows // 2 + 1, rows // 2
    full, h_a, mask_a = call(
        functools.partial(first_kernel, places, len(pieces), (0, cut_a)),
        pieces + [w1],
        [((rows, c, w), BF), act(cut_a), act(cut_a)],
        [wide],
        0,
        "first_conv_a",
    )
    h = {"a0": h_a, "a1": to_mate(h_a), "a2": over_x(h_a)}
    gy = over_y(v["g4"])
    h |= {"m1": to_mate(v["mate"]), "near3": to_mate(v["near"][1:])}
    h["gy"] = gy
    h_b, mask_b, flat = call(
        functools.partial(first_rest_kernel, (cut_a, rows)),
        [full, w1],
        [act(rows - cut_a)] * 2 + [((c, rows * w), BF)],
        [wide],
        0,
        "first_conv_b",
    )
    b1, b2 = to_mate(h_b), over_x(h_b)
    h |= {"b0": h_b}
    h = wave(h)
    h |= {"b2": b2, "b1": b1}
    cuts = [(n, min(n + 2, cut_a)) for n in range(0, cut_a, 2)]
    layout_a = [(e, 0, "whole") for e in range(3)] + [(3, n, "whole") for n, _ in cuts]
    spread_a = [h["a0"], h["a1"], h["a2"]] + [to_mate(h["a2"][n:m]) for n, m in cuts]
    grads = [v["g4"], h["gy"]]
    grad_places = [(p, k, z ^ p) for p in (0, 1) for k, z in enumerate(zs)]

    def second(layout, spread, part, before, early, name):
        n = part[1] - part[0]
        return call(
            functools.partial(second_kernel, grad_places, layout, len(grads), part, rows),
            [*spread, full, *grads, w2_wide, before],
            [act(1), act(n)] + [act(n // 2)] * early,
            [wide, vm((min(part[1] + 1, rows) - max(part[0] - 1, 0), c, w), BF), vm((rows, own, w), BF)],
            0,
            name,
        )

    s = {"b0": h["b0"], "b1": h["b1"], "b2": h["b2"], "far": over_y(lax.optimization_barrier((v["near"], gy))[0])}
    s["out"], gs_a, early = second(layout_a, spread_a, (0, cut), feat, 1, "second_conv_a")
    (s["terms"],) = call(
        functools.partial(second_terms_kernel, layout_a, (0, cut), 0),
        [*spread_a, gs_a],
        [((3, 3 * own, c), F32)],
        [vm((c, cut_a * w), BF), vm((3 * own, cut * w), BF)],
        0,
        "second_terms_a",
    )
    s = wave(s)
    n_b = rows - cut_a
    layout_b = layout_a + [(e, cut_a, "whole") for e in range(3)] + [(3, cut_a + n, "whole") for n in range(n_b)]
    spread_b = spread_a + [s["b0"], s["b1"], s["b2"]] + [to_mate(s["b2"][n : n + 1]) for n in range(n_b)]
    t = {"a0": gs_a, "s2": over_x(early), "a1": to_mate(gs_a), "far3": to_mate(s["far"][1:])}
    t["out"], t["b0"] = second(layout_b, spread_b, (cut, rows), s["out"], 0, "second_conv_b")
    b2 = over_x(t["b0"])
    t = wave(t)
    t |= {"b1": to_mate(t["b0"]), "t2": over_y(t["s2"]), "s3": to_mate(t["s2"])}

    (second_grad,) = call(
        functools.partial(second_terms_kernel, layout_b, (cut, rows), 1),
        [*spread_b, t["b0"], s["terms"]],
        [((3, 3 * own, c), F32)],
        [vm((c, rows * w), BF), vm((3 * own, (rows - cut) * w), BF)],
        0,
        "second_terms_b",
    )
    t["t2"], second_grad = lax.optimization_barrier((t["t2"], second_grad))
    t["t3"] = to_mate(t["t2"])
    last = cut - 1
    layout = [(e, 0, "whole") for e in (0, 1)] + [(e, 0, kind) for kind in ("own", "other") for e in (2, 3)]
    names = ["a0", "a1", "s2", "s3", "t2", "t3"]
    turned = [w2_taps, h["m1"], v["near"][:1], h["near3"], s["far"][:1], t["far3"]]
    (wide_back,) = call(turn_kernel, turned, [((3 * own, 3 * c), BF)], [], 0, "turn_weight")
    (grad_first,) = call(
        functools.partial(back_kernel, layout, (0, last), rows, (0,)),
        [*(t[k] for k in names), wide_back, mask_a],
        [act(last)],
        [vm((cut, c, w), BF)],
        0,
        "hidden_grad_a",
    )
    (terms,) = call(
        functools.partial(first_terms_kernel, (0, last)),
        [flat, grad_first],
        [((3, 3 * own, c), F32)],
        [vm((3 * own, last * w), BF)],
        0,
        "first_terms_a",
    )
    t |= {"b2": b2, "terms": terms, "wide": wide_back, "grad": second_grad}
    t = wave(t)
    layout += [(e, cut, "whole") for e in range(4)]
    (grad_first,) = call(
        functools.partial(back_kernel, layout, (last, rows), rows, (0, cut_a)),
        [*(t[k] for k in names), t["b0"], t["b1"], t["b2"], to_mate(t["b2"]), t["wide"], mask_a, mask_b],
        [act(rows - last)],
        [vm((rows - last + 1, c, w), BF)],
        row_flops * (rows - last),
        "hidden_grad_b",
    )
    (first_grad,) = call(
        functools.partial(first_terms_rest_kernel, (last, rows)),
        [flat, grad_first, t["terms"]],
        [((3, 3 * own, c), F32)],
        [vm((3 * own, (rows - last) * w), BF), vm((3, 3 * own, c), F32), DMA((3,))],
        row_flops * (rows - last),
        "first_terms_b",
        out_spec=ANY,
    )

    def as_weight(value):
        return jnp.transpose(value.reshape(3, 3, own, c), (2, 0, 1, 3))

    return jnp.transpose(t["out"], (1, 0, 2)), as_weight(first_grad), as_weight(t["grad"])


def solution(mesh):
    in_specs = (
        P("filt", "rows", None),
        P("filt", None, None, None),
        P("filt", None, None, None),
        P("filt", "rows", None),
    )
    out_specs = (P("filt", "rows", None), P("filt", None, None, None), P("filt", None, None, None))

    def per_device(features, first_weight, second_weight, out_grad):
        rows, filt = mesh.shape["rows"], mesh.shape["filt"]
        small = rows == 8 and filt == 4 and features.shape[1] == 1 and features.shape[0] % 32 == 0
        plan = all_rows if small else split_rows
        return plan(features, first_weight, second_weight, out_grad)

    return jax.shard_map(per_device, mesh=mesh, in_specs=in_specs, out_specs=out_specs, check_vma=False)
```

```python
import functools

import jax
import jax.numpy as jnp
from jax import lax
from jax.experimental import pallas as pl
from jax.experimental.pallas import tpu as pltpu
from jax.sharding import PartitionSpec as P

BF = jnp.bfloat16
F32 = jnp.float32
VMEM_BYTES = 24 * 1024 * 1024


def extended(cells, sides, width):
    for axis, dim in sides:
        count = lax.axis_size(axis)
        ends = count - 1
        head = lax.slice_in_dim(cells, 0, width, axis=dim)
        tail = lax.slice_in_dim(cells, cells.shape[dim] - width, cells.shape[dim], axis=dim)
        cells = jnp.concatenate(
            [
                lax.ppermute(tail, axis, [(i, (i + 1) % count) for i in range(ends)]),
                cells,
                lax.ppermute(head, axis, [((i + 1) % count, i) for i in range(ends)]),
            ],
            axis=dim,
        )
    return cells


def shift_cols(value, offset):
    if offset == 0:
        return value
    if offset > 0:
        return jnp.pad(value[..., offset:], ((0, 0), (0, 0), (0, offset)))
    return jnp.pad(value[..., :offset], ((0, 0), (0, 0), (-offset, 0)))


def conv_forward(weight, padded, count):
    total = jnp.zeros((weight.shape[0], count, padded.shape[2]), F32)
    for a in range(3):
        for b in range(3):
            part = jnp.einsum(
                "oi,ihw->ohw", weight[:, a, b, :], padded[:, a : a + count, :], preferred_element_type=F32
            )
            total = total + shift_cols(part, b - 1)
    return total


def conv_backward(weight, padded, count):
    total = jnp.zeros((weight.shape[3], count, padded.shape[2]), F32)
    for a in range(3):
        for b in range(3):
            part = jnp.einsum(
                "oi,ohw->ihw", weight[:, a, b, :], padded[:, 2 - a : 2 - a + count, :], preferred_element_type=F32
            )
            total = total + shift_cols(part, 1 - b)
    return total


def weight_terms(grad, padded, count):
    rows_out = []
    for a in range(3):
        cols_out = []
        for b in range(3):
            moved = shift_cols(grad, 1 - b)
            cols_out.append(
                jnp.einsum("ohw,ihw->oi", moved, padded[:, a : a + count, :], preferred_element_type=F32)
            )
        rows_out.append(jnp.stack(cols_out, axis=1))
    return jnp.stack(rows_out, axis=1)


def with_rims(value):
    return extended(value, (("rows", 1),), 1)


def all_channels(value):
    return lax.all_gather(with_rims(value), "filt", axis=0, tiled=True)


def split_rows(features, first_weight, second_weight, out_grad):
    count = features.shape[1]
    padded_in = all_channels(features)
    pre_first = conv_forward(first_weight, padded_in, count)
    hidden = jnp.maximum(pre_first, 0.0).astype(BF)
    padded_hidden = all_channels(hidden)
    pre_second = conv_forward(second_weight, padded_hidden, count) + features.astype(F32)
    block_out = jnp.maximum(pre_second, 0.0).astype(BF)
    grad_second = jnp.where(pre_second > 0, out_grad.astype(F32), 0.0).astype(BF)
    rimmed_grad = with_rims(grad_second)
    terms = conv_backward(second_weight, rimmed_grad, count)
    hidden_grad = lax.psum_scatter(terms, "filt", scatter_dimension=0, tiled=True)
    grad_first = jnp.where(pre_first > 0, hidden_grad, 0.0).astype(BF)
    second_local = weight_terms(grad_second, padded_hidden, count)
    first_local = weight_terms(grad_first, padded_in, count)
    first_grad, second_grad = lax.psum((first_local, second_local), "rows")
    return (block_out, first_grad, second_grad)


def swap(value, axis, bits):
    if axis == "filt":
        way = "mate" if bits == 1 else "over_x"
    else:
        way = "over_y" if bits == 1 else "along_z"
    with jax.named_scope(way):
        return lax.ppermute(value, axis, [(i, i ^ bits) for i in range(lax.axis_size(axis))])


def block_at(index, size):
    return pl.ds(pl.multiple_of(index * size, size), size)


def join_cols(left, mid, right):
    w = mid.shape[1]
    col = lax.broadcasted_iota(jnp.int32, mid.shape, 1)
    out = mid + jnp.where(col == 0, 0.0, pltpu.roll(left, 1, 1))
    return out + jnp.where(col == w - 1, 0.0, pltpu.roll(right, w - 1, 1))


def window(weight, x, r, rows, lo):
    c, w = x.shape[1], x.shape[2]
    first, last = max(r - 1, 0), min(r + 1, rows - 1)
    lhs = weight[:, (first - r + 1) * c : (last - r + 2) * c]
    rhs = x[first - lo : last - lo + 1].reshape((last - first + 1) * c, w)
    return jnp.dot(lhs, rhs, preferred_element_type=F32)


def thirds(acc):
    own = acc.shape[0] // 3
    return acc[:own], acc[own : 2 * own], acc[2 * own :]


def widen(weight, wide):
    c = weight.shape[2]
    for a in range(3):
        wide[:, a * c : (a + 1) * c] = weight[a]


def gather_rows(full, places, pieces):
    own = pieces[0].shape[1]
    r0, f0 = lax.axis_index("rows"), lax.axis_index("filt")
    for piece, k, d, e, lo in places:
        size = pieces[piece].shape[1]
        at = pl.ds(pl.multiple_of((f0 ^ e) * own + lo, size), size)
        full[r0 ^ d, at] = pieces[piece][k]


def first_rows(part, full, wide, hidden, mask):
    for r in range(*part):
        pre = join_cols(*thirds(window(wide, full, r, full.shape[0], 0)))
        hidden[r - part[0]] = jnp.maximum(pre, 0.0).astype(BF)
        mask[r - part[0]] = jnp.where(pre > 0, 1.0, 0.0).astype(BF)


def store_early(early, value, n, y0):
    count = early.shape[0]

    @pl.when(y0 == n // count)
    def _():
        early[n % count] = value


def first_kernel(places, n_pieces, part, *refs):
    pieces, weight = refs[:n_pieces], refs[n_pieces]
    full, hidden, mask, wide = refs[n_pieces + 1 :]
    gather_rows(full, places, pieces)
    widen(weight, wide)
    first_rows(part, full, wide, hidden, mask)


def first_rest_kernel(part, full, weight, hidden, mask, flat, wide):
    widen(weight, wide)
    first_rows(part, full, wide, hidden, mask)
    rows, _, w = full.shape
    for r in range(rows):
        flat[:, r * w : (r + 1) * w] = full[r]


def copy_pieces(layout, refs, put, lo, hi):
    y0, f0 = lax.axis_index("rows") & 1, lax.axis_index("filt")
    for (e, base, kind), ref in zip(layout, refs):
        count, own = ref.shape[:2]
        at = block_at(f0 ^ e, own)
        for n in range(count):
            if kind == "whole":
                if lo <= base + n < hi:
                    put(base + n, at, ref[n])
                continue
            half = y0 if kind == "own" else 1 - y0
            for y in (0, 1):
                if lo <= base + y * count + n < hi:

                    @pl.when(half == y)
                    def _(ref=ref, n=n, y=y, at=at):
                        put(base + y * count + n, at, ref[n])


def fill_rows(x, layout, refs, lo, hi):
    def put(r, at, value):
        x[r - lo, at] = value

    copy_pieces(layout, refs, put, lo, hi)


def second_kernel(grad_places, layout, n_grad, part, rows, *refs):
    pieces, refs = refs[: len(layout)], refs[len(layout) :]
    full, grads, weight, before = refs[0], refs[1 : 1 + n_grad], refs[1 + n_grad], refs[2 + n_grad]
    block_out, grad_second, *early, wide, x, grad = refs[3 + n_grad :]
    own = grad_second.shape[1]
    r0, f0 = lax.axis_index("rows"), lax.axis_index("filt")
    y0 = r0 & 1
    lo, hi = max(part[0] - 1, 0), min(part[1] + 1, rows)
    fill_rows(x, layout, pieces, lo, hi)
    for piece, k, d in grad_places:
        grad[r0 ^ d] = grads[piece][k]
    widen(weight, wide)
    block_out[...] = before[...]
    for r in range(*part):
        feat = full[r, block_at(f0, own)].astype(F32)
        pre = join_cols(*thirds(window(wide, x, r, rows, lo))) + feat
        value = jnp.where(pre > 0, grad[r].astype(F32), 0.0).astype(BF)
        grad_second[r - part[0]] = value
        if early:
            store_early(early[0], value, r - part[0], y0)

        @pl.when(r0 == r)
        def _(pre=pre):
            block_out[0] = jnp.maximum(pre, 0.0).astype(BF)


def hold_kernel(value, out):
    out[...] = value[...]


def pick_kernel(weight, mate, over, sems):
    own, half = mate.shape[1], over.shape[2]
    f0, y0 = lax.axis_index("filt"), lax.axis_index("rows") & 1
    copies = [pltpu.make_async_copy(weight.at[:, :, block_at(f0 ^ 1, own)], mate, sems.at[0])]
    for e in (2, 3):
        part = weight.at[:, block_at(y0, half), block_at(f0 ^ e, own)]
        copies.append(pltpu.make_async_copy(part, over.at[e - 2], sems.at[e - 1]))
    for copy in copies:
        copy.start()
    for copy in copies:
        copy.wait()


def turn_kernel(weight, mate, near2, near3, far2, far3, wide):
    own, half = mate.shape[1], near2.shape[2]
    c = wide.shape[1] // 3
    f0, y0 = lax.axis_index("filt"), lax.axis_index("rows") & 1
    for t in range(weight.shape[0]):
        a, b = t // 3, t % 3
        left = jnp.concatenate([near2[0, t], far2[0, t]], axis=0), jnp.concatenate([near3[0, t], far3[0, t]], axis=0)
        right = jnp.concatenate([far2[0, t], near2[0, t]], axis=0), jnp.concatenate([far3[0, t], near3[0, t]], axis=0)
        blocks = [weight[t, :, block_at(f0, own)], mate[t]]
        blocks += [jnp.where(y0 == 0, x, y) for x, y in zip(left, right)]
        for e, block in enumerate(blocks):
            at = pl.ds(pl.multiple_of((2 - a) * c + (f0 ^ e) * own, own), own)
            wide[b * own : (b + 1) * own, at] = block.T


def back_rows(part, rows, lo, x, wide, masks, grad_first):
    for r in range(*part):
        left, mid, right = thirds(window(wide, x, r, rows, lo))
        total = join_cols(right, mid, left)
        (mask,) = [ref[r - base] for base, ref in masks if 0 <= r - base < ref.shape[0]]
        grad_first[r - part[0]] = jnp.where(mask > 0, total, 0.0).astype(BF)


def back_kernel(layout, part, rows, bases, *refs):
    pieces, (wide, *masks, grad_first, x) = refs[: len(layout)], refs[len(layout) :]
    lo, hi = max(part[0] - 1, 0), min(part[1] + 1, rows)
    fill_rows(x, layout, pieces, lo, hi)
    back_rows(part, rows, lo, x, wide, list(zip(bases, masks)), grad_first)


def fill_moved(grads, moved):
    own, w = grads[0].shape[1:]
    col = lax.broadcasted_iota(jnp.int32, (own, w), 1)
    for r, (grad, n) in enumerate((grad, n) for grad in grads for n in range(grad.shape[0])):
        g = grad[n].astype(F32)
        at = slice(r * w, (r + 1) * w)
        moved[0:own, at] = jnp.where(col == w - 1, 0.0, pltpu.roll(g, w - 1, 1)).astype(BF)
        moved[own : 2 * own, at] = grad[n]
        moved[2 * own :, at] = jnp.where(col == 0, 0.0, pltpu.roll(g, 1, 1)).astype(BF)


def sum_terms(moved, x, w, a, part):
    rows = x.shape[1] // w
    lo, hi = max(part[0], 1 - a), min(part[1], rows + 1 - a)
    left, right = moved[:, (lo - part[0]) * w : (hi - part[0]) * w], x[:, (lo + a - 1) * w : (hi + a - 1) * w]
    return lax.dot_general(left, right, (((1,), (1,)), ((), ())), preferred_element_type=F32)


def second_terms_kernel(layout, part, with_before, *refs):
    pieces, (grad, *refs) = refs[: len(layout)], refs[len(layout) :]
    out, x, moved = refs[with_before:]
    w = grad.shape[2]

    def put(r, at, value):
        x[at, r * w : (r + 1) * w] = value

    copy_pieces(layout, pieces, put, max(part[0] - 1, 0), min(part[1] + 1, x.shape[1] // w))
    fill_moved([grad], moved)
    for a in range(3):
        terms = sum_terms(moved, x, w, a, part)
        out[a] = refs[0][a] + terms if with_before else terms


def first_terms_kernel(part, flat, grad, out, moved):
    fill_moved([grad], moved)
    for a in range(3):
        out[a] = sum_terms(moved, flat, grad.shape[2], a, part)


def first_terms_rest_kernel(part, flat, grad, before, out, moved, total, sems):
    fill_moved([grad], moved)
    copies = []
    for a in range(3):
        total[a] = before[a] + sum_terms(moved, flat, grad.shape[2], a, part)
        copies.append(pltpu.make_async_copy(total.at[a], out.at[a], sems.at[a]))
        copies[-1].start()
    for copy in copies:
        copy.wait()


VM = pl.BlockSpec(memory_space=pltpu.VMEM)
ANY = pl.BlockSpec(memory_space=pl.ANY)
DMA = pltpu.SemaphoreType.DMA


def call(kernel, ins, outs, scratch, flops, name, in_spec=VM, out_spec=VM):
    nbytes = sum(v.size * v.dtype.itemsize for v in ins) if flops else 0
    return pl.pallas_call(
        kernel,
        out_shape=[jax.ShapeDtypeStruct(s, d) for s, d in outs],
        in_specs=[in_spec] * len(ins),
        out_specs=[out_spec] * len(outs),
        scratch_shapes=scratch,
        compiler_params=pltpu.CompilerParams(vmem_limit_bytes=VMEM_BYTES),
        cost_estimate=pl.CostEstimate(flops=flops, bytes_accessed=nbytes, transcendentals=0),
        name=name,
    )(*ins)


def wave(values):
    return dict(zip(values, lax.optimization_barrier(tuple(values.values()))))


def over_x(value):
    return swap(value, "filt", 2)


def over_y(value):
    return swap(value, "rows", 1)


def to_mate(value):
    return swap(value, "filt", 1)


def all_rows(features, first_weight, second_weight, out_grad):
    c = first_weight.shape[3]
    own, _, w = features.shape
    rows = lax.axis_size("rows")
    half, cut = own // 2, rows // 2
    row_flops = 2 * 9 * own * c * w
    vm = pltpu.VMEM
    zs = tuple(range(2, rows, 2))
    wide = vm((3 * own, 3 * c), BF)
    w1 = jnp.transpose(first_weight, (1, 2, 0, 3)).reshape(3, 3 * own, c)
    w2 = jnp.transpose(second_weight, (1, 2, 0, 3))
    w2_wide = w2.reshape(3, 3 * own, c)
    feat = jnp.transpose(features, (1, 0, 2))
    ograd = jnp.transpose(out_grad, (1, 0, 2))

    def act(n):
        return ((n, own, w), BF)

    v = {f"z{d}": swap(feat, "rows", d) for d in zs[::-1]}
    w2_taps = w2.reshape(9, own, c)
    mate, over = call(
        pick_kernel,
        [w2_taps],
        [((9, own, own), BF), ((2, 9, half, own), BF)],
        [DMA((3,))],
        0,
        "pick_weight",
        in_spec=ANY,
    )
    (feat_near,) = call(hold_kernel, [feat], [act(1)], [], row_flops * 2, "hold_row")
    v |= {"mate": mate, "near": over_x(over), "feat": feat_near}
    v = wave(v)

    zs = (0, *zs)
    z4 = jnp.concatenate([v["feat"]] + [v[f"z{d}"] for d in zs[1:]], axis=0)
    v |= {f"g{d}": swap(ograd, "rows", d) for d in zs[:0:-1]}
    v |= {"z4": z4, "x4": over_x(z4), "y4": over_y(z4)}
    v = wave(v)

    v |= {"lo": over_y(v["x4"][:, :half]), "hi": over_x(v["y4"][:, half:])}
    v |= {"m" + k: to_mate(v[k]) for k in ("z4", "x4", "y4")}
    v |= {"g4": jnp.concatenate([ograd] + [v[f"g{d}"] for d in zs[1:]], axis=0)}
    v = wave(v)
    v |= {"mlo": to_mate(v["lo"]), "mhi": to_mate(v["hi"])}
    v = wave(v)

    pieces, places = [], []
    for name, d, e, lo in (("z4", 0, 0, 0), ("x4", 0, 2, 0), ("y4", 1, 0, 0), ("lo", 1, 2, 0), ("hi", 1, 2, half)):
        for core in (0, 1):
            places += [(len(pieces), k, z ^ d, e ^ core, lo) for k, z in enumerate(zs)]
            pieces.append(v["m" * core + name])
    cut_a, cut = rows // 2 + 1, rows // 2
    full, h_a, mask_a = call(
        functools.partial(first_kernel, places, len(pieces), (0, cut_a)),
        pieces + [w1],
        [((rows, c, w), BF), act(cut_a), act(cut_a)],
        [wide],
        0,
        "first_conv_a",
    )
    h = {"a0": h_a, "a1": to_mate(h_a), "a2": over_x(h_a)}
    gy = over_y(v["g4"])
    h |= {"m1": to_mate(v["mate"]), "near3": to_mate(v["near"][1:])}
    h["gy"] = gy
    h_b, mask_b, flat = call(
        functools.partial(first_rest_kernel, (cut_a, rows)),
        [full, w1],
        [act(rows - cut_a)] * 2 + [((c, rows * w), BF)],
        [wide],
        0,
        "first_conv_b",
    )
    b1, b2 = to_mate(h_b), over_x(h_b)
    h |= {"b0": h_b}
    h = wave(h)
    h |= {"b2": b2, "b1": b1}
    cuts = [(n, min(n + 2, cut_a)) for n in range(0, cut_a, 2)]
    layout_a = [(e, 0, "whole") for e in range(3)] + [(3, n, "whole") for n, _ in cuts]
    spread_a = [h["a0"], h["a1"], h["a2"]] + [to_mate(h["a2"][n:m]) for n, m in cuts]
    grads = [v["g4"], h["gy"]]
    grad_places = [(p, k, z ^ p) for p in (0, 1) for k, z in enumerate(zs)]

    def second(layout, spread, part, before, early, name):
        n = part[1] - part[0]
        return call(
            functools.partial(second_kernel, grad_places, layout, len(grads), part, rows),
            [*spread, full, *grads, w2_wide, before],
            [act(1), act(n)] + [act(n // 2)] * early,
            [wide, vm((min(part[1] + 1, rows) - max(part[0] - 1, 0), c, w), BF), vm((rows, own, w), BF)],
            0,
            name,
        )

    s = {"b0": h["b0"], "b1": h["b1"], "b2": h["b2"], "far": over_y(lax.optimization_barrier((v["near"], gy))[0])}
    s["out"], gs_a, early = second(layout_a, spread_a, (0, cut), feat, 1, "second_conv_a")
    (s["terms"],) = call(
        functools.partial(second_terms_kernel, layout_a, (0, cut), 0),
        [*spread_a, gs_a],
        [((3, 3 * own, c), F32)],
        [vm((c, cut_a * w), BF), vm((3 * own, cut * w), BF)],
        0,
        "second_terms_a",
    )
    s = wave(s)
    n_b = rows - cut_a
    layout_b = layout_a + [(e, cut_a, "whole") for e in range(3)] + [(3, cut_a + n, "whole") for n in range(n_b)]
    spread_b = spread_a + [s["b0"], s["b1"], s["b2"]] + [to_mate(s["b2"][n : n + 1]) for n in range(n_b)]
    t = {"a0": gs_a, "s2": over_x(early), "a1": to_mate(gs_a), "far3": to_mate(s["far"][1:])}
    t["out"], t["b0"] = second(layout_b, spread_b, (cut, rows), s["out"], 0, "second_conv_b")
    b2 = over_x(t["b0"])
    t = wave(t)
    t |= {"b1": to_mate(t["b0"]), "t2": over_y(t["s2"]), "s3": to_mate(t["s2"])}

    (second_grad,) = call(
        functools.partial(second_terms_kernel, layout_b, (cut, rows), 1),
        [*spread_b, t["b0"], s["terms"]],
        [((3, 3 * own, c), F32)],
        [vm((c, rows * w), BF), vm((3 * own, (rows - cut) * w), BF)],
        0,
        "second_terms_b",
    )
    t["t2"], second_grad = lax.optimization_barrier((t["t2"], second_grad))
    t["t3"] = to_mate(t["t2"])
    last = cut - 1
    layout = [(e, 0, "whole") for e in (0, 1)] + [(e, 0, kind) for kind in ("own", "other") for e in (2, 3)]
    names = ["a0", "a1", "s2", "s3", "t2", "t3"]
    turned = [w2_taps, h["m1"], v["near"][:1], h["near3"], s["far"][:1], t["far3"]]
    (wide_back,) = call(turn_kernel, turned, [((3 * own, 3 * c), BF)], [], 0, "turn_weight")
    (grad_first,) = call(
        functools.partial(back_kernel, layout, (0, last), rows, (0,)),
        [*(t[k] for k in names), wide_back, mask_a],
        [act(last)],
        [vm((cut, c, w), BF)],
        0,
        "hidden_grad_a",
    )
    (terms,) = call(
        functools.partial(first_terms_kernel, (0, last)),
        [flat, grad_first],
        [((3, 3 * own, c), F32)],
        [vm((3 * own, last * w), BF)],
        0,
        "first_terms_a",
    )
    t |= {"b2": b2, "terms": terms, "wide": wide_back, "grad": second_grad}
    t = wave(t)
    layout += [(e, cut, "whole") for e in range(4)]
    (grad_first,) = call(
        functools.partial(back_kernel, layout, (last, rows), rows, (0, cut_a)),
        [*(t[k] for k in names), t["b0"], t["b1"], t["b2"], to_mate(t["b2"]), t["wide"], mask_a, mask_b],
        [act(rows - last)],
        [vm((rows - last + 1, c, w), BF)],
        row_flops * (rows - last),
        "hidden_grad_b",
    )
    (first_grad,) = call(
        functools.partial(first_terms_rest_kernel, (last, rows)),
        [flat, grad_first, t["terms"]],
        [((3, 3 * own, c), F32)],
        [vm((3 * own, (rows - last) * w), BF), vm((3, 3 * own, c), F32), DMA((3,))],
        row_flops * (rows - last),
        "first_terms_b",
        out_spec=ANY,
    )

    def as_weight(value):
        return jnp.transpose(value.reshape(3, 3, own, c), (2, 0, 1, 3))

    return jnp.transpose(t["out"], (1, 0, 2)), as_weight(first_grad), as_weight(t["grad"])


def solution(mesh):
    in_specs = (
        P("filt", "rows", None),
        P("filt", None, None, None),
        P("filt", None, None, None),
        P("filt", "rows", None),
    )
    out_specs = (P("filt", "rows", None), P("filt", None, None, None), P("filt", None, None, None))

    def per_device(features, first_weight, second_weight, out_grad):
        rows, filt = mesh.shape["rows"], mesh.shape["filt"]
        small = rows == 8 and filt == 4 and features.shape[1] == 1 and features.shape[0] % 32 == 0
        plan = all_rows if small else split_rows
        return plan(features, first_weight, second_weight, out_grad)

    return jax.shard_map(per_device, mesh=mesh, in_specs=in_specs, out_specs=out_specs, check_vma=False)
```

```python
import functools

import jax
import jax.numpy as jnp
from jax import lax
from jax.experimental import pallas as pl
from jax.experimental.pallas import tpu as pltpu
from jax.sharding import PartitionSpec as P

BF = jnp.bfloat16
F32 = jnp.float32
VMEM_BYTES = 24 * 1024 * 1024


def extended(cells, sides, width):
    for axis, dim in sides:
        count = lax.axis_size(axis)
        ends = count - 1
        head = lax.slice_in_dim(cells, 0, width, axis=dim)
        tail = lax.slice_in_dim(cells, cells.shape[dim] - width, cells.shape[dim], axis=dim)
        cells = jnp.concatenate(
            [
                lax.ppermute(tail, axis, [(i, (i + 1) % count) for i in range(ends)]),
                cells,
                lax.ppermute(head, axis, [((i + 1) % count, i) for i in range(ends)]),
            ],
            axis=dim,
        )
    return cells


def shift_cols(value, offset):
    if offset == 0:
        return value
    if offset > 0:
        return jnp.pad(value[..., offset:], ((0, 0), (0, 0), (0, offset)))
    return jnp.pad(value[..., :offset], ((0, 0), (0, 0), (-offset, 0)))


def conv_forward(weight, padded, count):
    total = jnp.zeros((weight.shape[0], count, padded.shape[2]), F32)
    for a in range(3):
        for b in range(3):
            part = jnp.einsum(
                "oi,ihw->ohw", weight[:, a, b, :], padded[:, a : a + count, :], preferred_element_type=F32
            )
            total = total + shift_cols(part, b - 1)
    return total


def conv_backward(weight, padded, count):
    total = jnp.zeros((weight.shape[3], count, padded.shape[2]), F32)
    for a in range(3):
        for b in range(3):
            part = jnp.einsum(
                "oi,ohw->ihw", weight[:, a, b, :], padded[:, 2 - a : 2 - a + count, :], preferred_element_type=F32
            )
            total = total + shift_cols(part, 1 - b)
    return total


def weight_terms(grad, padded, count):
    rows_out = []
    for a in range(3):
        cols_out = []
        for b in range(3):
            moved = shift_cols(grad, 1 - b)
            cols_out.append(
                jnp.einsum("ohw,ihw->oi", moved, padded[:, a : a + count, :], preferred_element_type=F32)
            )
        rows_out.append(jnp.stack(cols_out, axis=1))
    return jnp.stack(rows_out, axis=1)


def with_rims(value):
    return extended(value, (("rows", 1),), 1)


def all_channels(value):
    return lax.all_gather(with_rims(value), "filt", axis=0, tiled=True)


def split_rows(features, first_weight, second_weight, out_grad):
    count = features.shape[1]
    padded_in = all_channels(features)
    pre_first = conv_forward(first_weight, padded_in, count)
    hidden = jnp.maximum(pre_first, 0.0).astype(BF)
    padded_hidden = all_channels(hidden)
    pre_second = conv_forward(second_weight, padded_hidden, count) + features.astype(F32)
    block_out = jnp.maximum(pre_second, 0.0).astype(BF)
    grad_second = jnp.where(pre_second > 0, out_grad.astype(F32), 0.0).astype(BF)
    rimmed_grad = with_rims(grad_second)
    terms = conv_backward(second_weight, rimmed_grad, count)
    hidden_grad = lax.psum_scatter(terms, "filt", scatter_dimension=0, tiled=True)
    grad_first = jnp.where(pre_first > 0, hidden_grad, 0.0).astype(BF)
    second_local = weight_terms(grad_second, padded_hidden, count)
    first_local = weight_terms(grad_first, padded_in, count)
    first_grad, second_grad = lax.psum((first_local, second_local), "rows")
    return (block_out, first_grad, second_grad)


def swap(value, axis, bits):
    if axis == "filt":
        way = "mate" if bits == 1 else "over_x"
    else:
        way = "over_y" if bits == 1 else "along_z"
    with jax.named_scope(way):
        return lax.ppermute(value, axis, [(i, i ^ bits) for i in range(lax.axis_size(axis))])


def block_at(index, size):
    return pl.ds(pl.multiple_of(index * size, size), size)


def join_cols(left, mid, right):
    w = mid.shape[1]
    col = lax.broadcasted_iota(jnp.int32, mid.shape, 1)
    out = mid + jnp.where(col == 0, 0.0, pltpu.roll(left, 1, 1))
    return out + jnp.where(col == w - 1, 0.0, pltpu.roll(right, w - 1, 1))


def window(weight, x, r, rows, lo):
    c, w = x.shape[1], x.shape[2]
    first, last = max(r - 1, 0), min(r + 1, rows - 1)
    lhs = weight[:, (first - r + 1) * c : (last - r + 2) * c]
    rhs = x[first - lo : last - lo + 1].reshape((last - first + 1) * c, w)
    return jnp.dot(lhs, rhs, preferred_element_type=F32)


def thirds(acc):
    own = acc.shape[0] // 3
    return acc[:own], acc[own : 2 * own], acc[2 * own :]


def widen(weight, wide):
    c = weight.shape[2]
    for a in range(3):
        wide[:, a * c : (a + 1) * c] = weight[a]


def gather_rows(full, places, pieces):
    own = pieces[0].shape[1]
    r0, f0 = lax.axis_index("rows"), lax.axis_index("filt")
    for piece, k, d, e, lo in places:
        size = pieces[piece].shape[1]
        at = pl.ds(pl.multiple_of((f0 ^ e) * own + lo, size), size)
        full[r0 ^ d, at] = pieces[piece][k]


def first_rows(part, full, wide, hidden, mask):
    for r in range(*part):
        pre = join_cols(*thirds(window(wide, full, r, full.shape[0], 0)))
        hidden[r - part[0]] = jnp.maximum(pre, 0.0).astype(BF)
        mask[r - part[0]] = jnp.where(pre > 0, 1.0, 0.0).astype(BF)


def store_early(early, value, n, y0):
    count = early.shape[0]

    @pl.when(y0 == n // count)
    def _():
        early[n % count] = value


def first_kernel(places, n_pieces, part, *refs):
    pieces, weight = refs[:n_pieces], refs[n_pieces]
    full, hidden, mask, wide = refs[n_pieces + 1 :]
    gather_rows(full, places, pieces)
    widen(weight, wide)
    first_rows(part, full, wide, hidden, mask)


def first_rest_kernel(part, full, weight, hidden, mask, *refs):
    *flats, wide = refs
    widen(weight, wide)
    first_rows(part, full, wide, hidden, mask)
    rows, _, w = full.shape
    for flat in flats:
        for r in range(rows):
            flat[:, r * w : (r + 1) * w] = full[r]


def copy_pieces(layout, refs, put, lo, hi):
    y0, f0 = lax.axis_index("rows") & 1, lax.axis_index("filt")
    others = {(e, base): ref for (e, base, kind), ref in zip(layout, refs) if kind == "other"}
    for (e, base, kind), ref in zip(layout, refs):
        count, own = ref.shape[:2]
        at = block_at(f0 ^ e, own)
        for n in range(count):
            if kind == "whole" and lo <= base + n < hi:
                put(base + n, at, ref[n])
            for y in (0, 1):
                if kind == "own" and lo <= base + y * count + n < hi:
                    put(base + y * count + n, at, jnp.where(y0 == y, ref[n], others[e, base][n]))


def fill_rows(x, layout, refs, lo, hi):
    def put(r, at, value):
        x[r - lo, at] = value

    copy_pieces(layout, refs, put, lo, hi)


def second_kernel(grad_places, layout, n_grad, part, rows, *refs):
    pieces, refs = refs[: len(layout)], refs[len(layout) :]
    full, grads, weight, before = refs[0], refs[1 : 1 + n_grad], refs[1 + n_grad], refs[2 + n_grad]
    block_out, grad_second, *early, wide, x, grad = refs[3 + n_grad :]
    own = grad_second.shape[1]
    r0, f0 = lax.axis_index("rows"), lax.axis_index("filt")
    y0 = r0 & 1
    lo, hi = max(part[0] - 1, 0), min(part[1] + 1, rows)
    fill_rows(x, layout, pieces, lo, hi)
    for piece, k, d in grad_places:
        grad[r0 ^ d] = grads[piece][k]
    widen(weight, wide)
    block_out[...] = before[...]
    for r in range(*part):
        feat = full[r, block_at(f0, own)].astype(F32)
        pre = join_cols(*thirds(window(wide, x, r, rows, lo))) + feat
        value = jnp.where(pre > 0, grad[r].astype(F32), 0.0).astype(BF)
        grad_second[r - part[0]] = value
        if early:
            store_early(early[0], value, r - part[0], y0)

        @pl.when(r0 == r)
        def _(pre=pre):
            block_out[0] = jnp.maximum(pre, 0.0).astype(BF)


def hold_kernel(value, out):
    out[...] = value[...]


def pick_kernel(weight, mate, over, sems):
    own, half = mate.shape[1], over.shape[2]
    f0, y0 = lax.axis_index("filt"), lax.axis_index("rows") & 1
    copies = [pltpu.make_async_copy(weight.at[:, :, block_at(f0 ^ 1, own)], mate, sems.at[0])]
    for e in (2, 3):
        part = weight.at[:, block_at(y0, half), block_at(f0 ^ e, own)]
        copies.append(pltpu.make_async_copy(part, over.at[e - 2], sems.at[e - 1]))
    for copy in copies:
        copy.start()
    for copy in copies:
        copy.wait()


def turn_kernel(weight, mate, near2, near3, far2, far3, wide):
    own, half = mate.shape[1], near2.shape[2]
    c = wide.shape[1] // 3
    f0, y0 = lax.axis_index("filt"), lax.axis_index("rows") & 1
    for t in range(weight.shape[0]):
        a, b = t // 3, t % 3
        left = jnp.concatenate([near2[0, t], far2[0, t]], axis=0), jnp.concatenate([near3[0, t], far3[0, t]], axis=0)
        right = jnp.concatenate([far2[0, t], near2[0, t]], axis=0), jnp.concatenate([far3[0, t], near3[0, t]], axis=0)
        blocks = [weight[t, :, block_at(f0, own)], mate[t]]
        blocks += [jnp.where(y0 == 0, x, y) for x, y in zip(left, right)]
        for e, block in enumerate(blocks):
            at = pl.ds(pl.multiple_of((2 - a) * c + (f0 ^ e) * own, own), own)
            wide[b * own : (b + 1) * own, at] = block.T


def back_rows(part, rows, lo, x, wide, masks, grad_first):
    for r in range(*part):
        left, mid, right = thirds(window(wide, x, r, rows, lo))
        total = join_cols(right, mid, left)
        (mask,) = [ref[r - base] for base, ref in masks if 0 <= r - base < ref.shape[0]]
        grad_first[r - part[0]] = jnp.where(mask > 0, total, 0.0).astype(BF)


def back_kernel(layout, part, rows, bases, *refs):
    pieces, (wide, *masks, grad_first, x) = refs[: len(layout)], refs[len(layout) :]
    lo, hi = max(part[0] - 1, 0), min(part[1] + 1, rows)
    fill_rows(x, layout, pieces, lo, hi)
    back_rows(part, rows, lo, x, wide, list(zip(bases, masks)), grad_first)


def fill_moved(grads, moved):
    own, w = grads[0].shape[1:]
    col = lax.broadcasted_iota(jnp.int32, (own, w), 1)
    for r, (grad, n) in enumerate((grad, n) for grad in grads for n in range(grad.shape[0])):
        g = grad[n].astype(F32)
        at = slice(r * w, (r + 1) * w)
        moved[0:own, at] = jnp.where(col == w - 1, 0.0, pltpu.roll(g, w - 1, 1)).astype(BF)
        moved[own : 2 * own, at] = grad[n]
        moved[2 * own :, at] = jnp.where(col == 0, 0.0, pltpu.roll(g, 1, 1)).astype(BF)


def sum_terms(moved, x, w, a, part):
    rows = x.shape[1] // w
    lo, hi = max(part[0], 1 - a), min(part[1], rows + 1 - a)
    left, right = moved[:, (lo - part[0]) * w : (hi - part[0]) * w], x[:, (lo + a - 1) * w : (hi + a - 1) * w]
    return lax.dot_general(left, right, (((1,), (1,)), ((), ())), preferred_element_type=F32)


def second_terms_kernel(layout, part, with_before, *refs):
    pieces, (grad, *refs) = refs[: len(layout)], refs[len(layout) :]
    out, x, moved = refs[with_before:]
    w = grad.shape[2]

    def put(r, at, value):
        x[at, r * w : (r + 1) * w] = value

    copy_pieces(layout, pieces, put, max(part[0] - 1, 0), min(part[1] + 1, x.shape[1] // w))
    fill_moved([grad], moved)
    for a in range(3):
        terms = sum_terms(moved, x, w, a, part)
        out[a] = refs[0][a] + terms if with_before else terms


def first_terms_kernel(part, flat, grad, out, moved):
    fill_moved([grad], moved)
    for a in range(3):
        out[a] = sum_terms(moved, flat, grad.shape[2], a, part)


def last_kernel(layout, part, rows, bases, *refs):
    pieces, refs = refs[: len(layout)], refs[len(layout) :]
    wide, mask_m, mask_b, flat, before, out, x, grad, moved, total, sems = refs
    lo, hi = max(part[0] - 1, 0), min(part[1] + 1, rows)
    fill_rows(x, layout, pieces, lo, hi)
    back_rows(part, rows, lo, x, wide, list(zip(bases, (mask_m, mask_b))), grad)
    fill_moved([grad], moved)
    copies = []
    for a in range(3):
        total[a] = before[a] + sum_terms(moved, flat, grad.shape[2], a, part)
        copies.append(pltpu.make_async_copy(total.at[a], out.at[a], sems.at[a]))
        copies[-1].start()
    for copy in copies:
        copy.wait()


VM = pl.BlockSpec(memory_space=pltpu.VMEM)
ANY = pl.BlockSpec(memory_space=pl.ANY)
DMA = pltpu.SemaphoreType.DMA


def call(kernel, ins, outs, scratch, flops, name, in_spec=VM, out_spec=VM):
    nbytes = sum(v.size * v.dtype.itemsize for v in ins) if flops else 0
    return pl.pallas_call(
        kernel,
        out_shape=[jax.ShapeDtypeStruct(s, d) for s, d in outs],
        in_specs=[in_spec] * len(ins),
        out_specs=[out_spec] * len(outs),
        scratch_shapes=scratch,
        compiler_params=pltpu.CompilerParams(vmem_limit_bytes=VMEM_BYTES),
        cost_estimate=pl.CostEstimate(flops=flops, bytes_accessed=nbytes, transcendentals=0),
        name=name,
    )(*ins)


def wave(values):
    return dict(zip(values, lax.optimization_barrier(tuple(values.values()))))


def over_x(value):
    return swap(value, "filt", 2)


def over_y(value):
    return swap(value, "rows", 1)


def to_mate(value):
    return swap(value, "filt", 1)


def all_rows(features, first_weight, second_weight, out_grad):
    c = first_weight.shape[3]
    own, _, w = features.shape
    rows = lax.axis_size("rows")
    half, cut = own // 2, rows // 2
    row_flops = 2 * 9 * own * c * w
    vm = pltpu.VMEM
    zs = tuple(range(2, rows, 2))
    wide = vm((3 * own, 3 * c), BF)
    w1 = jnp.transpose(first_weight, (1, 2, 0, 3)).reshape(3, 3 * own, c)
    w2 = jnp.transpose(second_weight, (1, 2, 0, 3))
    w2_wide = w2.reshape(3, 3 * own, c)
    feat = jnp.transpose(features, (1, 0, 2))
    ograd = jnp.transpose(out_grad, (1, 0, 2))

    def act(n):
        return ((n, own, w), BF)

    v = {f"z{d}": swap(feat, "rows", d) for d in zs[::-1]}
    w2_taps = w2.reshape(9, own, c)
    mate, over = call(
        pick_kernel,
        [w2_taps],
        [((9, own, own), BF), ((2, 9, half, own), BF)],
        [DMA((3,))],
        0,
        "pick_weight",
        in_spec=ANY,
    )
    (feat_near,) = call(hold_kernel, [feat], [act(1)], [], row_flops * 2, "hold_row")
    v |= {"mate": mate, "near": over_x(over), "feat": feat_near}
    v = wave(v)

    zs = (0, *zs)
    z4 = jnp.concatenate([v["feat"]] + [v[f"z{d}"] for d in zs[1:]], axis=0)
    v |= {f"g{d}": swap(ograd, "rows", d) for d in zs[:0:-1]}
    v |= {"z4": z4, "x4": over_x(z4), "y4": over_y(z4)}
    v = wave(v)

    v |= {"lo": over_y(v["x4"][:, :half]), "hi": over_x(v["y4"][:, half:])}
    v |= {"m" + k: to_mate(v[k]) for k in ("z4", "x4", "y4")}
    v |= {"g4": jnp.concatenate([ograd] + [v[f"g{d}"] for d in zs[1:]], axis=0)}
    v = wave(v)
    v |= {"mlo": to_mate(v["lo"]), "mhi": to_mate(v["hi"])}
    v = wave(v)

    pieces, places = [], []
    for name, d, e, lo in (("z4", 0, 0, 0), ("x4", 0, 2, 0), ("y4", 1, 0, 0), ("lo", 1, 2, 0), ("hi", 1, 2, half)):
        for core in (0, 1):
            places += [(len(pieces), k, z ^ d, e ^ core, lo) for k, z in enumerate(zs)]
            pieces.append(v["m" * core + name])
    cut_a, cut = rows // 2 + 1, rows // 2
    start = 2
    full, h_a, mask_a = call(
        functools.partial(first_kernel, places, len(pieces), (0, start)),
        pieces + [w1],
        [((rows, c, w), BF), act(start), act(start)],
        [wide],
        0,
        "first_conv_a",
    )

    def first_rest(part, with_flat, flops, name):
        return call(
            functools.partial(first_rest_kernel, part),
            [full, w1],
            [act(part[1] - part[0])] * 2 + [((c, rows * w), BF)] * with_flat,
            [wide],
            flops,
            name,
        )

    x0 = over_x(h_a)
    h_m, mask_m = first_rest((start, cut_a), 0, row_flops * 3, "first_conv_m")
    gy = over_y(v["g4"])
    h = {"h0": h_a, "h1": h_m, "x0": x0, "x1": over_x(h_m), "m0": to_mate(h_a), "m1": to_mate(h_m), "gy": gy}
    h |= {"mate": to_mate(v["mate"]), "near3": to_mate(v["near"][1:]), "xm0": to_mate(x0)}
    h_b, mask_b, flat = first_rest((cut_a, rows), 1, 0, "first_conv_b")
    b1, b2 = to_mate(h_b), over_x(h_b)
    h |= {"b0": h_b}
    h = wave(h)
    h |= {"b2": b2, "b1": b1}
    cuts = [(n, min(n + 2, cut_a)) for n in range(start, cut_a, 2)]
    layout_a = [(e, 0, "whole") for e in range(4)] + [(e, start, "whole") for e in range(3)] + [(3, n, "whole") for n, _ in cuts]
    spread_a = [h[k] for k in ("h0", "m0", "x0", "xm0", "h1", "m1", "x1")]
    spread_a += [to_mate(h["x1"][n - start : m - start]) for n, m in cuts]
    grads = [v["g4"], h["gy"]]
    grad_places = [(p, k, z ^ p) for p in (0, 1) for k, z in enumerate(zs)]

    def second(layout, spread, part, before, early, name):
        n = part[1] - part[0]
        return call(
            functools.partial(second_kernel, grad_places, layout, len(grads), part, rows),
            [*spread, full, *grads, w2_wide, before],
            [act(1), act(n)] + [act(n // 2)] * early,
            [wide, vm((min(part[1] + 1, rows) - max(part[0] - 1, 0), c, w), BF), vm((rows, own, w), BF)],
            0,
            name,
        )

    s = {"b0": h["b0"], "b1": h["b1"], "b2": h["b2"], "far": over_y(lax.optimization_barrier((v["near"], gy))[0])}
    s["out"], gs_a, early = second(layout_a, spread_a, (0, cut), feat, 1, "second_conv_a")
    (s["terms"],) = call(
        functools.partial(second_terms_kernel, layout_a, (0, cut), 0),
        [*spread_a, gs_a],
        [((3, 3 * own, c), F32)],
        [vm((c, cut_a * w), BF), vm((3 * own, cut * w), BF)],
        0,
        "second_terms_a",
    )
    s = wave(s)
    n_b = rows - cut_a
    layout_b = layout_a + [(e, cut_a, "whole") for e in range(3)] + [(3, cut_a + n, "whole") for n in range(n_b)]
    spread_b = spread_a + [s["b0"], s["b1"], s["b2"]] + [to_mate(s["b2"][n : n + 1]) for n in range(n_b)]
    t = {"a0": gs_a, "s2": over_x(early), "a1": to_mate(gs_a), "far3": to_mate(s["far"][1:])}
    t["out"], t["b0"] = second(layout_b, spread_b, (cut, rows), s["out"], 0, "second_conv_b")
    b2 = over_x(t["b0"])
    t = wave(t)
    t |= {"b1": to_mate(t["b0"]), "t2": over_y(t["s2"]), "s3": to_mate(t["s2"])}

    (second_grad,) = call(
        functools.partial(second_terms_kernel, layout_b, (cut, rows), 1),
        [*spread_b, t["b0"], s["terms"]],
        [((3, 3 * own, c), F32)],
        [vm((c, rows * w), BF), vm((3 * own, (rows - cut) * w), BF)],
        0,
        "second_terms_b",
    )
    t["t2"], second_grad = lax.optimization_barrier((t["t2"], second_grad))
    t["t3"] = to_mate(t["t2"])
    last = cut - 1
    layout = [(e, 0, "whole") for e in (0, 1)] + [(e, 0, kind) for kind in ("own", "other") for e in (2, 3)]
    names = ["a0", "a1", "s2", "s3", "t2", "t3"]
    turned = [w2_taps, h["mate"], v["near"][:1], h["near3"], s["far"][:1], t["far3"]]
    (wide_back,) = call(turn_kernel, turned, [((3 * own, 3 * c), BF)], [], 0, "turn_weight")
    (grad_first,) = call(
        functools.partial(back_kernel, layout, (0, last), rows, (0, start)),
        [*(t[k] for k in names), wide_back, mask_a, mask_m],
        [act(last)],
        [vm((cut, c, w), BF)],
        0,
        "hidden_grad_a",
    )
    (terms,) = call(
        functools.partial(first_terms_kernel, (0, last)),
        [flat, grad_first],
        [((3, 3 * own, c), F32)],
        [vm((3 * own, last * w), BF)],
        0,
        "first_terms_a",
    )
    t |= {"b2": b2, "terms": terms, "wide": wide_back, "grad": second_grad}
    t = wave(t)
    layout += [(e, cut, "whole") for e in range(4)]
    n = rows - last
    (first_grad,) = call(
        functools.partial(last_kernel, layout, (last, rows), rows, (start, cut_a)),
        [*(t[k] for k in names), t["b0"], t["b1"], t["b2"], to_mate(t["b2"]), t["wide"], mask_m, mask_b, flat, t["terms"]],
        [((3, 3 * own, c), F32)],
        [
            vm((n + 1, c, w), BF),
            vm((n, own, w), BF),
            vm((3 * own, n * w), BF),
            vm((3, 3 * own, c), F32),
            DMA((3,)),
        ],
        2 * row_flops * n,
        "hidden_grad_b_first_terms_b",
        out_spec=ANY,
    )

    def as_weight(value):
        return jnp.transpose(value.reshape(3, 3, own, c), (2, 0, 1, 3))

    return jnp.transpose(t["out"], (1, 0, 2)), as_weight(first_grad), as_weight(t["grad"])


def solution(mesh):
    in_specs = (
        P("filt", "rows", None),
        P("filt", None, None, None),
        P("filt", None, None, None),
        P("filt", "rows", None),
    )
    out_specs = (P("filt", "rows", None), P("filt", None, None, None), P("filt", None, None, None))

    def per_device(features, first_weight, second_weight, out_grad):
        rows, filt = mesh.shape["rows"], mesh.shape["filt"]
        small = rows == 8 and filt == 4 and features.shape[1] == 1 and features.shape[0] % 32 == 0
        plan = all_rows if small else split_rows
        return plan(features, first_weight, second_weight, out_grad)

    return jax.shard_map(per_device, mesh=mesh, in_specs=in_specs, out_specs=out_specs, check_vma=False)
```

```python
import functools

import jax
import jax.numpy as jnp
from jax import lax
from jax.experimental import pallas as pl
from jax.experimental.pallas import tpu as pltpu
from jax.sharding import PartitionSpec as P

BF = jnp.bfloat16
F32 = jnp.float32
VMEM_BYTES = 24 * 1024 * 1024


def extended(cells, sides, width):
    for axis, dim in sides:
        count = lax.axis_size(axis)
        ends = count - 1
        head = lax.slice_in_dim(cells, 0, width, axis=dim)
        tail = lax.slice_in_dim(cells, cells.shape[dim] - width, cells.shape[dim], axis=dim)
        cells = jnp.concatenate(
            [
                lax.ppermute(tail, axis, [(i, (i + 1) % count) for i in range(ends)]),
                cells,
                lax.ppermute(head, axis, [((i + 1) % count, i) for i in range(ends)]),
            ],
            axis=dim,
        )
    return cells


def shift_cols(value, offset):
    if offset == 0:
        return value
    if offset > 0:
        return jnp.pad(value[..., offset:], ((0, 0), (0, 0), (0, offset)))
    return jnp.pad(value[..., :offset], ((0, 0), (0, 0), (-offset, 0)))


def conv_forward(weight, padded, count):
    total = jnp.zeros((weight.shape[0], count, padded.shape[2]), F32)
    for a in range(3):
        for b in range(3):
            part = jnp.einsum(
                "oi,ihw->ohw", weight[:, a, b, :], padded[:, a : a + count, :], preferred_element_type=F32
            )
            total = total + shift_cols(part, b - 1)
    return total


def conv_backward(weight, padded, count):
    total = jnp.zeros((weight.shape[3], count, padded.shape[2]), F32)
    for a in range(3):
        for b in range(3):
            part = jnp.einsum(
                "oi,ohw->ihw", weight[:, a, b, :], padded[:, 2 - a : 2 - a + count, :], preferred_element_type=F32
            )
            total = total + shift_cols(part, 1 - b)
    return total


def weight_terms(grad, padded, count):
    rows_out = []
    for a in range(3):
        cols_out = []
        for b in range(3):
            moved = shift_cols(grad, 1 - b)
            cols_out.append(
                jnp.einsum("ohw,ihw->oi", moved, padded[:, a : a + count, :], preferred_element_type=F32)
            )
        rows_out.append(jnp.stack(cols_out, axis=1))
    return jnp.stack(rows_out, axis=1)


def with_rims(value):
    return extended(value, (("rows", 1),), 1)


def all_channels(value):
    return lax.all_gather(with_rims(value), "filt", axis=0, tiled=True)


def split_rows(features, first_weight, second_weight, out_grad):
    count = features.shape[1]
    padded_in = all_channels(features)
    pre_first = conv_forward(first_weight, padded_in, count)
    hidden = jnp.maximum(pre_first, 0.0).astype(BF)
    padded_hidden = all_channels(hidden)
    pre_second = conv_forward(second_weight, padded_hidden, count) + features.astype(F32)
    block_out = jnp.maximum(pre_second, 0.0).astype(BF)
    grad_second = jnp.where(pre_second > 0, out_grad.astype(F32), 0.0).astype(BF)
    rimmed_grad = with_rims(grad_second)
    terms = conv_backward(second_weight, rimmed_grad, count)
    hidden_grad = lax.psum_scatter(terms, "filt", scatter_dimension=0, tiled=True)
    grad_first = jnp.where(pre_first > 0, hidden_grad, 0.0).astype(BF)
    second_local = weight_terms(grad_second, padded_hidden, count)
    first_local = weight_terms(grad_first, padded_in, count)
    first_grad, second_grad = lax.psum((first_local, second_local), "rows")
    return (block_out, first_grad, second_grad)


def swap(value, axis, bits):
    if axis == "filt":
        way = "mate" if bits == 1 else "over_x"
    else:
        way = "over_y" if bits == 1 else "along_z"
    with jax.named_scope(way):
        return lax.ppermute(value, axis, [(i, i ^ bits) for i in range(lax.axis_size(axis))])


def block_at(index, size):
    return pl.ds(pl.multiple_of(index * size, size), size)


def join_cols(left, mid, right):
    w = mid.shape[1]
    col = lax.broadcasted_iota(jnp.int32, mid.shape, 1)
    out = mid + jnp.where(col == 0, 0.0, pltpu.roll(left, 1, 1))
    return out + jnp.where(col == w - 1, 0.0, pltpu.roll(right, w - 1, 1))


def window(weight, x, r, rows, lo):
    c, w = x.shape[1], x.shape[2]
    first, last = max(r - 1, 0), min(r + 1, rows - 1)
    lhs = weight[:, (first - r + 1) * c : (last - r + 2) * c]
    rhs = x[first - lo : last - lo + 1].reshape((last - first + 1) * c, w)
    return jnp.dot(lhs, rhs, preferred_element_type=F32)


def thirds(acc):
    own = acc.shape[0] // 3
    return acc[:own], acc[own : 2 * own], acc[2 * own :]


def widen(weight, wide):
    c = weight.shape[2]
    for a in range(3):
        wide[:, a * c : (a + 1) * c] = weight[a]


def gather_rows(full, places, pieces):
    own = pieces[0].shape[1]
    r0, f0 = lax.axis_index("rows"), lax.axis_index("filt")
    for piece, k, d, e, lo in places:
        size = pieces[piece].shape[1]
        at = pl.ds(pl.multiple_of((f0 ^ e) * own + lo, size), size)
        full[r0 ^ d, at] = pieces[piece][k]


def first_rows(part, full, wide, hidden, mask):
    for r in range(*part):
        pre = join_cols(*thirds(window(wide, full, r, full.shape[0], 0)))
        hidden[r - part[0]] = jnp.maximum(pre, 0.0).astype(BF)
        mask[r - part[0]] = jnp.where(pre > 0, 1.0, 0.0).astype(BF)


def store_early(early, value, n, y0):
    count = early.shape[0]

    @pl.when(y0 == n // count)
    def _():
        early[n % count] = value


def first_kernel(places, n_pieces, part, *refs):
    pieces, weight = refs[:n_pieces], refs[n_pieces]
    full, hidden, mask, wide = refs[n_pieces + 1 :]
    gather_rows(full, places, pieces)
    widen(weight, wide)
    first_rows(part, full, wide, hidden, mask)


def first_rest_kernel(part, full, weight, hidden, mask, *refs):
    *flats, wide = refs
    widen(weight, wide)
    first_rows(part, full, wide, hidden, mask)
    rows, _, w = full.shape
    for flat in flats:
        for r in range(rows):
            flat[:, r * w : (r + 1) * w] = full[r]


def copy_pieces(layout, refs, put, lo, hi):
    y0, f0 = lax.axis_index("rows") & 1, lax.axis_index("filt")
    others = {(e, base): ref for (e, base, kind), ref in zip(layout, refs) if kind == "other"}
    for (e, base, kind), ref in zip(layout, refs):
        count, own = ref.shape[:2]
        at = block_at(f0 ^ e, own)
        for n in range(count):
            if kind == "whole" and lo <= base + n < hi:
                put(base + n, at, ref[n])
            for y in (0, 1):
                if kind == "own" and lo <= base + y * count + n < hi:
                    put(base + y * count + n, at, jnp.where(y0 == y, ref[n], others[e, base][n]))


def fill_rows(x, layout, refs, lo, hi):
    def put(r, at, value):
        x[r - lo, at] = value

    copy_pieces(layout, refs, put, lo, hi)


def second_kernel(grad_places, layout, n_grad, part, rows, *refs):
    pieces, refs = refs[: len(layout)], refs[len(layout) :]
    full, grads, weight, before = refs[0], refs[1 : 1 + n_grad], refs[1 + n_grad], refs[2 + n_grad]
    block_out, grad_second, *early, wide, x, grad = refs[3 + n_grad :]
    own = grad_second.shape[1]
    r0, f0 = lax.axis_index("rows"), lax.axis_index("filt")
    y0 = r0 & 1
    lo, hi = max(part[0] - 1, 0), min(part[1] + 1, rows)
    fill_rows(x, layout, pieces, lo, hi)
    for piece, k, d in grad_places:
        grad[r0 ^ d] = grads[piece][k]
    widen(weight, wide)
    block_out[...] = before[...]
    for r in range(*part):
        feat = full[r, block_at(f0, own)].astype(F32)
        pre = join_cols(*thirds(window(wide, x, r, rows, lo))) + feat
        value = jnp.where(pre > 0, grad[r].astype(F32), 0.0).astype(BF)
        grad_second[r - part[0]] = value
        if early:
            store_early(early[0], value, r - part[0], y0)

        @pl.when(r0 == r)
        def _(pre=pre):
            block_out[0] = jnp.maximum(pre, 0.0).astype(BF)


def hold_kernel(value, out):
    out[...] = value[...]


def pick_kernel(weight, mate, over, sems):
    own, half = mate.shape[1], over.shape[2]
    f0, y0 = lax.axis_index("filt"), lax.axis_index("rows") & 1
    copies = [pltpu.make_async_copy(weight.at[:, :, block_at(f0 ^ 1, own)], mate, sems.at[0])]
    for e in (2, 3):
        part = weight.at[:, block_at(y0, half), block_at(f0 ^ e, own)]
        copies.append(pltpu.make_async_copy(part, over.at[e - 2], sems.at[e - 1]))
    for copy in copies:
        copy.start()
    for copy in copies:
        copy.wait()


def turn_kernel(weight, mate, near2, near3, far2, far3, wide):
    own, half = mate.shape[1], near2.shape[2]
    c = wide.shape[1] // 3
    f0, y0 = lax.axis_index("filt"), lax.axis_index("rows") & 1
    for t in range(weight.shape[0]):
        a, b = t // 3, t % 3
        left = jnp.concatenate([near2[0, t], far2[0, t]], axis=0), jnp.concatenate([near3[0, t], far3[0, t]], axis=0)
        right = jnp.concatenate([far2[0, t], near2[0, t]], axis=0), jnp.concatenate([far3[0, t], near3[0, t]], axis=0)
        blocks = [weight[t, :, block_at(f0, own)], mate[t]]
        blocks += [jnp.where(y0 == 0, x, y) for x, y in zip(left, right)]
        for e, block in enumerate(blocks):
            at = pl.ds(pl.multiple_of((2 - a) * c + (f0 ^ e) * own, own), own)
            wide[b * own : (b + 1) * own, at] = block.T


def back_rows(part, rows, lo, x, wide, masks, grad_first):
    for r in range(*part):
        left, mid, right = thirds(window(wide, x, r, rows, lo))
        total = join_cols(right, mid, left)
        (mask,) = [ref[r - base] for base, ref in masks if 0 <= r - base < ref.shape[0]]
        grad_first[r - part[0]] = jnp.where(mask > 0, total, 0.0).astype(BF)


def back_kernel(layout, part, rows, bases, *refs):
    pieces, (wide, *masks, grad_first, x) = refs[: len(layout)], refs[len(layout) :]
    lo, hi = max(part[0] - 1, 0), min(part[1] + 1, rows)
    fill_rows(x, layout, pieces, lo, hi)
    back_rows(part, rows, lo, x, wide, list(zip(bases, masks)), grad_first)


def fill_moved(grads, moved):
    own, w = grads[0].shape[1:]
    col = lax.broadcasted_iota(jnp.int32, (own, w), 1)
    for r, (grad, n) in enumerate((grad, n) for grad in grads for n in range(grad.shape[0])):
        g = grad[n].astype(F32)
        at = slice(r * w, (r + 1) * w)
        moved[0:own, at] = jnp.where(col == w - 1, 0.0, pltpu.roll(g, w - 1, 1)).astype(BF)
        moved[own : 2 * own, at] = grad[n]
        moved[2 * own :, at] = jnp.where(col == 0, 0.0, pltpu.roll(g, 1, 1)).astype(BF)


def sum_terms(moved, x, w, a, part):
    rows = x.shape[1] // w
    lo, hi = max(part[0], 1 - a), min(part[1], rows + 1 - a)
    left, right = moved[:, (lo - part[0]) * w : (hi - part[0]) * w], x[:, (lo + a - 1) * w : (hi + a - 1) * w]
    return lax.dot_general(left, right, (((1,), (1,)), ((), ())), preferred_element_type=F32)


def second_terms_kernel(layout, part, with_before, *refs):
    pieces, (grad, *refs) = refs[: len(layout)], refs[len(layout) :]
    out, x, moved = refs[with_before:]
    w = grad.shape[2]

    def put(r, at, value):
        x[at, r * w : (r + 1) * w] = value

    copy_pieces(layout, pieces, put, max(part[0] - 1, 0), min(part[1] + 1, x.shape[1] // w))
    fill_moved([grad], moved)
    for a in range(3):
        terms = sum_terms(moved, x, w, a, part)
        out[a] = refs[0][a] + terms if with_before else terms


def first_terms_kernel(part, flat, grad, out, moved):
    fill_moved([grad], moved)
    for a in range(3):
        out[a] = sum_terms(moved, flat, grad.shape[2], a, part)


def fill_kernel(layout, lo, hi, *refs):
    fill_rows(refs[-1], layout, refs[:-1], lo, hi)


def last_kernel(layout, part, rows, bases, *refs):
    pieces, refs = refs[: len(layout)], refs[len(layout) :]
    wide, mask_m, mask_b, flat, before, _, out, x, grad, moved, total, sems = refs
    lo, hi = max(part[0] - 1, 0), min(part[1] + 1, rows)
    fill_rows(x, layout, pieces, lo, hi)
    back_rows(part, rows, lo, x, wide, list(zip(bases, (mask_m, mask_b))), grad)
    fill_moved([grad], moved)
    copies = []
    for a in range(3):
        total[a] = before[a] + sum_terms(moved, flat, grad.shape[2], a, part)
        copies.append(pltpu.make_async_copy(total.at[a], out.at[a], sems.at[a]))
        copies[-1].start()
    for copy in copies:
        copy.wait()


VM = pl.BlockSpec(memory_space=pltpu.VMEM)
ANY = pl.BlockSpec(memory_space=pl.ANY)
DMA = pltpu.SemaphoreType.DMA


def call(kernel, ins, outs, scratch, flops, name, in_spec=VM, out_spec=VM, aliases=None):
    nbytes = sum(v.size * v.dtype.itemsize for v in ins) if flops else 0
    return pl.pallas_call(
        kernel,
        out_shape=[jax.ShapeDtypeStruct(s, d) for s, d in outs],
        in_specs=[in_spec] * len(ins),
        out_specs=[out_spec] + [VM] * (len(outs) - 1),
        input_output_aliases=aliases or {},
        scratch_shapes=scratch,
        compiler_params=pltpu.CompilerParams(vmem_limit_bytes=VMEM_BYTES),
        cost_estimate=pl.CostEstimate(flops=flops, bytes_accessed=nbytes, transcendentals=0),
        name=name,
    )(*ins)


def wave(values):
    return dict(zip(values, lax.optimization_barrier(tuple(values.values()))))


def over_x(value):
    return swap(value, "filt", 2)


def over_y(value):
    return swap(value, "rows", 1)


def to_mate(value):
    return swap(value, "filt", 1)


def all_rows(features, first_weight, second_weight, out_grad):
    c = first_weight.shape[3]
    own, _, w = features.shape
    rows = lax.axis_size("rows")
    half, cut = own // 2, rows // 2
    row_flops = 2 * 9 * own * c * w
    vm = pltpu.VMEM
    zs = tuple(range(2, rows, 2))
    wide = vm((3 * own, 3 * c), BF)
    w1 = jnp.transpose(first_weight, (1, 2, 0, 3)).reshape(3, 3 * own, c)
    w2 = jnp.transpose(second_weight, (1, 2, 0, 3))
    w2_wide = w2.reshape(3, 3 * own, c)
    feat = jnp.transpose(features, (1, 0, 2))
    ograd = jnp.transpose(out_grad, (1, 0, 2))

    def act(n):
        return ((n, own, w), BF)

    v = {f"z{d}": swap(feat, "rows", d) for d in zs[::-1]}
    w2_taps = w2.reshape(9, own, c)
    mate, over = call(
        pick_kernel,
        [w2_taps],
        [((9, own, own), BF), ((2, 9, half, own), BF)],
        [DMA((3,))],
        0,
        "pick_weight",
        in_spec=ANY,
    )
    (feat_near,) = call(hold_kernel, [feat], [act(1)], [], row_flops * 2, "hold_row")
    v |= {"mate": mate, "near": over_x(over), "feat": feat_near}
    v = wave(v)

    zs = (0, *zs)
    z4 = jnp.concatenate([v["feat"]] + [v[f"z{d}"] for d in zs[1:]], axis=0)
    v |= {f"g{d}": swap(ograd, "rows", d) for d in zs[:0:-1]}
    v |= {"z4": z4, "x4": over_x(z4), "y4": over_y(z4)}
    v = wave(v)

    v |= {"lo": over_y(v["x4"][:, :half]), "hi": over_x(v["y4"][:, half:])}
    v |= {"m" + k: to_mate(v[k]) for k in ("z4", "x4", "y4")}
    v |= {"g4": jnp.concatenate([ograd] + [v[f"g{d}"] for d in zs[1:]], axis=0)}
    v = wave(v)
    v |= {"mlo": to_mate(v["lo"]), "mhi": to_mate(v["hi"])}
    v = wave(v)

    pieces, places = [], []
    for name, d, e, lo in (("z4", 0, 0, 0), ("x4", 0, 2, 0), ("y4", 1, 0, 0), ("lo", 1, 2, 0), ("hi", 1, 2, half)):
        for core in (0, 1):
            places += [(len(pieces), k, z ^ d, e ^ core, lo) for k, z in enumerate(zs)]
            pieces.append(v["m" * core + name])
    cut_a, cut = rows // 2 + 1, rows // 2
    start = 2
    full, h_a, mask_a = call(
        functools.partial(first_kernel, places, len(pieces), (0, start)),
        pieces + [w1],
        [((rows, c, w), BF), act(start), act(start)],
        [wide],
        0,
        "first_conv_a",
    )

    def first_rest(part, with_flat, flops, name):
        return call(
            functools.partial(first_rest_kernel, part),
            [full, w1],
            [act(part[1] - part[0])] * 2 + [((c, rows * w), BF)] * with_flat,
            [wide],
            flops,
            name,
        )

    x0 = over_x(h_a)
    h_m, mask_m = first_rest((start, cut_a), 0, row_flops * 3, "first_conv_m")
    gy = over_y(v["g4"])
    h = {"h0": h_a, "h1": h_m, "x0": x0, "x1": over_x(h_m), "m0": to_mate(h_a), "m1": to_mate(h_m), "gy": gy}
    h |= {"mate": to_mate(v["mate"]), "near3": to_mate(v["near"][1:]), "xm0": to_mate(x0)}
    h_b, mask_b, flat = first_rest((cut_a, rows), 1, 0, "first_conv_b")
    b1, b2 = to_mate(h_b), over_x(h_b)
    h |= {"b0": h_b}
    h = wave(h)
    h |= {"b2": b2, "b1": b1}
    cuts = [(n, min(n + 2, cut_a)) for n in range(start, cut_a, 2)]
    layout_a = [(e, 0, "whole") for e in range(4)] + [(e, start, "whole") for e in range(3)] + [(3, n, "whole") for n, _ in cuts]
    spread_a = [h[k] for k in ("h0", "m0", "x0", "xm0", "h1", "m1", "x1")]
    spread_a += [to_mate(h["x1"][n - start : m - start]) for n, m in cuts]
    grads = [v["g4"], h["gy"]]
    grad_places = [(p, k, z ^ p) for p in (0, 1) for k, z in enumerate(zs)]

    def second(layout, spread, part, before, early, name):
        n = part[1] - part[0]
        return call(
            functools.partial(second_kernel, grad_places, layout, len(grads), part, rows),
            [*spread, full, *grads, w2_wide, before],
            [act(1), act(n)] + [act(n // 2)] * early,
            [wide, vm((min(part[1] + 1, rows) - max(part[0] - 1, 0), c, w), BF), vm((rows, own, w), BF)],
            0,
            name,
        )

    s = {"b0": h["b0"], "b1": h["b1"], "b2": h["b2"], "far": over_y(lax.optimization_barrier((v["near"], gy))[0])}
    s["out"], gs_a, early = second(layout_a, spread_a, (0, cut), feat, 1, "second_conv_a")
    (s["terms"],) = call(
        functools.partial(second_terms_kernel, layout_a, (0, cut), 0),
        [*spread_a, gs_a],
        [((3, 3 * own, c), F32)],
        [vm((c, cut_a * w), BF), vm((3 * own, cut * w), BF)],
        0,
        "second_terms_a",
    )
    s = wave(s)
    n_b = rows - cut_a
    layout_b = layout_a + [(e, cut_a, "whole") for e in range(3)] + [(3, cut_a + n, "whole") for n in range(n_b)]
    spread_b = spread_a + [s["b0"], s["b1"], s["b2"]] + [to_mate(s["b2"][n : n + 1]) for n in range(n_b)]
    t = {"a0": gs_a, "s2": over_x(early), "a1": to_mate(gs_a), "far3": to_mate(s["far"][1:])}
    t["out"], t["b0"] = second(layout_b, spread_b, (cut, rows), s["out"], 0, "second_conv_b")
    b2 = over_x(t["b0"])
    t = wave(t)
    t |= {"b1": to_mate(t["b0"]), "t2": over_y(t["s2"]), "s3": to_mate(t["s2"])}

    (second_grad,) = call(
        functools.partial(second_terms_kernel, layout_b, (cut, rows), 1),
        [*spread_b, t["b0"], s["terms"]],
        [((3, 3 * own, c), F32)],
        [vm((c, rows * w), BF), vm((3 * own, (rows - cut) * w), BF)],
        0,
        "second_terms_b",
    )
    t["t2"], second_grad = lax.optimization_barrier((t["t2"], second_grad))
    t["t3"] = to_mate(t["t2"])
    last = cut - 1
    layout = [(e, 0, "whole") for e in (0, 1)] + [(e, 0, kind) for kind in ("own", "other") for e in (2, 3)]
    names = ["a0", "a1", "s2", "s3", "t2", "t3"]
    turned = [w2_taps, h["mate"], v["near"][:1], h["near3"], s["far"][:1], t["far3"]]
    (wide_back,) = call(turn_kernel, turned, [((3 * own, 3 * c), BF)], [], 0, "turn_weight")
    (grad_first,) = call(
        functools.partial(back_kernel, layout, (0, last), rows, (0, start)),
        [*(t[k] for k in names), wide_back, mask_a, mask_m],
        [act(last)],
        [vm((cut, c, w), BF)],
        0,
        "hidden_grad_a",
    )
    (terms,) = call(
        functools.partial(first_terms_kernel, (0, last)),
        [flat, grad_first],
        [((3, 3 * own, c), F32)],
        [vm((3 * own, last * w), BF)],
        0,
        "first_terms_a",
    )
    n = rows - last
    known = layout + [(e, cut, "whole") for e in (0, 1)]
    (x,) = call(
        functools.partial(fill_kernel, known, last - 1, rows),
        [*(t[k] for k in names), t["b0"], t["b1"]],
        [((n + 1, c, w), BF)],
        [],
        0,
        "known_rows",
    )
    t |= {"b2": b2, "terms": terms, "wide": wide_back, "grad": second_grad, "x": x}
    t = wave(t)
    first_grad, _ = call(
        functools.partial(last_kernel, [(e, cut, "whole") for e in (2, 3)], (last, rows), rows, (start, cut_a)),
        [t["b2"], to_mate(t["b2"]), t["wide"], mask_m, mask_b, flat, t["terms"], t["x"]],
        [((3, 3 * own, c), F32), ((n + 1, c, w), BF)],
        [vm((n, own, w), BF), vm((3 * own, n * w), BF), vm((3, 3 * own, c), F32), DMA((3,))],
        2 * row_flops * n,
        "hidden_grad_b_first_terms_b",
        out_spec=ANY,
        aliases={7: 1},
    )

    def as_weight(value):
        return jnp.transpose(value.reshape(3, 3, own, c), (2, 0, 1, 3))

    return jnp.transpose(t["out"], (1, 0, 2)), as_weight(first_grad), as_weight(t["grad"])


def solution(mesh):
    in_specs = (
        P("filt", "rows", None),
        P("filt", None, None, None),
        P("filt", None, None, None),
        P("filt", "rows", None),
    )
    out_specs = (P("filt", "rows", None), P("filt", None, None, None), P("filt", None, None, None))

    def per_device(features, first_weight, second_weight, out_grad):
        rows, filt = mesh.shape["rows"], mesh.shape["filt"]
        small = rows == 8 and filt == 4 and features.shape[1] == 1 and features.shape[0] % 32 == 0
        plan = all_rows if small else split_rows
        return plan(features, first_weight, second_weight, out_grad)

    return jax.shard_map(per_device, mesh=mesh, in_specs=in_specs, out_specs=out_specs, check_vma=False)
```
